32 devices in a mesh: dp: 4 (over y, x), own: 8 (over z, core).
Axes of the slice: x: 2, y: 2, z: 4, core: 2. Of those that a mesh axis runs over, the one named last changes fastest.
Arguments:
- partial_grads: bfloat16 [4, 8, 512, 512], P('dp', None, 'own'), may hold values from -6 to 6
- owner_list: int32 [8], replicated, may hold values from 0 to 7, as said below
- left_stat: float32 [16, 512, 512], P('own', 'dp'), may hold values from -6 to 6
- right_stat: float32 [16, 512, 512], P('own', 'dp'), may hold values from -6 to 6
- left_root: bfloat16 [16, 512, 512], P('own', 'dp'), as said below
- right_root: bfloat16 [16, 512, 512], P('own', 'dp'), as said below
Outputs:
- new_left: float32 [16, 512, 512], P('own', 'dp')
- new_right: float32 [16, 512, 512], P('own', 'dp')
- update: bfloat16 [8, 512, 512], P(None, 'own', 'dp')
The draws below stay inside these ranges and needn't reach their ends.
Inputs may be any that keep to these rules, and one draw needn't show every extreme that they name: `owner_list`: each owner is named by at most 2 blocks; a quarter of the owners are named by exactly 2 blocks, half by one, a quarter by none. `left_root`: each matrix is symmetric and positive definite. `right_root`: each matrix is symmetric and positive definite.
All inputs are finite; a program needn't handle non-finite values.
Results may differ from the reference program's by a relative error of at most 0.015.
Values may be sent and summed in bfloat16 or wider, within the bound.
A program may use at most 64 MiB of HBM per device.

```python
import jax
import jax.numpy as jnp
from jax import lax

BLOCK = 512
CAP = 2
NBLK = 8
SLOTS = 16
N_DP = 4
N_OWN = 8


def draw_owner_list(key, part):
    key = jax.random.fold_in(key, 11)
    first_key, second_key = jax.random.split(key)
    owner_order = jax.random.permutation(first_key, N_OWN)
    blocks = jnp.arange(NBLK, dtype=jnp.int32)
    picked = jnp.where(blocks < NBLK // 2, blocks // 2, blocks - NBLK // 4)
    raw_owner = owner_order[picked]
    shuffle = jax.random.permutation(second_key, NBLK)
    return raw_owner[shuffle].astype(jnp.int32)


def symmetric_factor(key, ramp_low, ramp_high, jitter):
    noise_key, diag_key = jax.random.split(key)
    noise = jax.random.normal(noise_key, (SLOTS, BLOCK, BLOCK), jnp.float32)
    factor = jax.random.uniform(diag_key, (SLOTS, BLOCK, 1), jnp.float32, 1.0 - jitter, 1.0 + jitter)
    position = jnp.arange(BLOCK, dtype=jnp.float32)[None, :, None] / (BLOCK - 1.0)
    diagonal = (ramp_low + (ramp_high - ramp_low) * position) * factor
    mirrored = (noise + jnp.swapaxes(noise, 1, 2)) * (0.15 / BLOCK ** 0.5)
    identity = jnp.eye(BLOCK, dtype=jnp.float32)[None, :, :]
    return mirrored + identity * diagonal


def draw_left_root(key, part):
    key = jax.random.fold_in(key, 21)
    return symmetric_factor(key, 0.75, 2.5, 0.15).astype(jnp.bfloat16)


def draw_right_root(key, part):
    key = jax.random.fold_in(key, 22)
    return symmetric_factor(key, 0.75, 2.5, 0.15).astype(jnp.bfloat16)


def level_of(stream_key, shape, cuts, least, high):
    def one(axis_at, blocks):
        steps = jax.random.uniform(jax.random.fold_in(jax.random.fold_in(stream_key, 6), axis_at), (blocks,), jnp.float32, least / len(cuts), high / len(cuts))
        return jnp.repeat(jnp.exp(steps), shape[axis_at] // blocks).reshape((-1,) + (1,) * (len(shape) - axis_at - 1))

    loudness = one(*cuts[0])
    for cut in cuts[1:]:
        loudness = loudness * one(*cut)
    return loudness


def normal_values(rng, dims, width, limit, pieces=(), held_as=jnp.bfloat16):
    values = width * jax.random.normal(rng, dims, jnp.float32)
    if pieces:
        values = values * level_of(rng, dims, pieces, -0.22, 0.18)
    return jnp.clip(values, -limit, limit).astype(held_as)


def setup_inputs(seed: int = 0) -> dict:
    splits = jax.random.split(jax.random.key(seed), 7)
    partial_grads = normal_values(splits[0], (N_DP, NBLK, BLOCK, BLOCK), 1.0, 6.0, ((0, 4), (2, 8)))
    owner_list = draw_owner_list(jax.random.fold_in(splits[6], 71), 0)
    left_stat = normal_values(splits[2], (SLOTS, BLOCK, BLOCK), 1.0, 6.0, ((0, 8), (1, 4)), jnp.float32)
    right_stat = normal_values(splits[3], (SLOTS, BLOCK, BLOCK), 1.0, 6.0, ((0, 8), (1, 4)), jnp.float32)
    left_root = draw_left_root(jax.random.fold_in(splits[6], 71), 0)
    right_root = draw_right_root(jax.random.fold_in(splits[6], 71), 0)
    return {"partial_grads": partial_grads, "owner_list": owner_list, "left_stat": left_stat, "right_stat": right_stat, "left_root": left_root, "right_root": right_root}


decay_rate = 0.95
epsilon = 1e-06

def slot_numbers(owner_list):
    owner_hits = (owner_list[:, None] == jnp.arange(N_OWN, dtype=jnp.int32)[None, :]).astype(jnp.int32)
    before = jnp.cumsum(owner_hits, axis=0) - owner_hits
    return lax.optimization_barrier(jnp.sum(before * owner_hits, axis=1)).astype(jnp.int32)

def per_slot(slot_items):
    grad_block, slot_flag, left_old, right_old, left_factor, right_factor = slot_items
    left_gram = jnp.dot(grad_block, grad_block.T, preferred_element_type=jnp.float32)
    right_gram = jnp.dot(grad_block.T, grad_block, preferred_element_type=jnp.float32)
    left_next = jnp.where(slot_flag > 0, decay_rate * left_old + left_gram / BLOCK, left_old)
    right_next = jnp.where(slot_flag > 0, decay_rate * right_old + right_gram / BLOCK, right_old)
    half_done = jnp.dot(grad_block, right_factor, preferred_element_type=jnp.float32).astype(jnp.bfloat16)
    product = jnp.dot(left_factor, half_done, preferred_element_type=jnp.float32)
    cell_count = float(BLOCK * BLOCK)
    grad_sq = jnp.sum(jnp.square(grad_block.astype(jnp.float32)))
    prod_sq = jnp.sum(product * product)
    graft_ratio = jnp.sqrt(grad_sq / cell_count) / jnp.sqrt(prod_sq / cell_count + epsilon)
    return (left_next, right_next, (product * graft_ratio).astype(jnp.bfloat16))

def reference(partial_grads, owner_list, left_stat, right_stat, left_root, right_root):
    summed_grads = lax.optimization_barrier(jnp.sum(partial_grads.astype(jnp.float32), axis=0)).astype(jnp.bfloat16)
    slot_index = slot_numbers(owner_list)
    where_to = (owner_list * CAP + slot_index).astype(jnp.int32)
    placed = jnp.zeros((SLOTS, BLOCK, BLOCK), jnp.bfloat16).at[where_to].set(summed_grads)
    slot_used = jnp.zeros((SLOTS,), jnp.float32).at[where_to].set(1.0)
    new_left, new_right, slot_updates = lax.map(per_slot, (placed, slot_used, left_stat, right_stat, left_root, right_root))
    return (new_left, new_right, slot_updates[where_to])
```

```python
import functools

import jax
import jax.numpy as jnp
from jax import lax
from jax.experimental import pallas as pl
from jax.experimental.pallas import tpu as pltpu
from jax.sharding import PartitionSpec as P

decay_rate = 0.95
epsilon = 1e-06

MESH = pl.DeviceIdType.MESH
LANES = 128


def body(partial_grads, owner_list, left_stat, right_stat, left_root, right_root):
    owners = lax.axis_size("own")
    capacity = left_stat.shape[0]
    quarter = left_stat.shape[1]
    block_width = left_stat.shape[2]
    blocks = owner_list.shape[0]
    owner_hits = (owner_list[:, None] == jnp.arange(owners, dtype=jnp.int32)[None, :]).astype(
        jnp.int32
    )
    before = jnp.cumsum(owner_hits, axis=0) - owner_hits
    slot_index = jnp.sum(before * owner_hits, axis=1)
    slot_hits = (slot_index[:, None] == jnp.arange(capacity, dtype=jnp.int32)[None, :]).astype(
        jnp.int32
    )
    slot_match = slot_hits[:, :, None] * owner_hits[:, None, :]
    source_block = jnp.sum(slot_match * jnp.arange(blocks, dtype=jnp.int32)[:, None, None], axis=0)
    filled_flag = jnp.sum(slot_match, axis=0).astype(jnp.bfloat16)
    local_terms = partial_grads[0].astype(jnp.float32)
    shared = lax.psum(local_terms.astype(jnp.bfloat16), "dp")
    outgoing = jnp.take(shared, source_block, axis=0) * filled_flag[:, :, None, None]
    arrived = lax.all_to_all(outgoing, "own", split_axis=1, concat_axis=1, tiled=True)
    grad_part = arrived.reshape(capacity, block_width, arrived.shape[3])
    dp_lane = lax.axis_index("dp")
    own_index = lax.axis_index("own")
    owner_load = jnp.sum((owner_list == own_index).astype(jnp.int32))
    slot_used = (jnp.arange(capacity, dtype=jnp.int32) < owner_load)[:, None, None]
    row_start = dp_lane * quarter
    grad_rows = lax.dynamic_slice_in_dim(grad_part, row_start, quarter, 1)
    grad_colq = lax.dynamic_slice_in_dim(grad_part, row_start, quarter, 2)
    left_gram = jnp.einsum("cqk,cnk->cqn", grad_rows, grad_part, preferred_element_type=jnp.float32)
    right_gram = jnp.einsum(
        "ckq,ckn->cqn", grad_colq, grad_part, preferred_element_type=jnp.float32
    )
    new_left = jnp.where(slot_used, decay_rate * left_stat + left_gram / block_width, left_stat)
    new_right = jnp.where(slot_used, decay_rate * right_stat + right_gram / block_width, right_stat)
    half_done = jnp.einsum(
        "ckn,cqn->ckq", grad_part, right_root, preferred_element_type=jnp.float32
    ).astype(jnp.bfloat16)
    product = jnp.einsum(
        "cpn,cpq->cnq",
        lax.all_gather(left_root, "dp", axis=1, tiled=True),
        half_done,
        preferred_element_type=jnp.float32,
    )
    grad_sq = jnp.sum(jnp.square(grad_part.astype(jnp.float32)), axis=(1, 2))
    prod_sq = lax.psum(jnp.sum(product * product, axis=(1, 2)), "dp")
    cell_count = float(block_width * block_width)
    graft_ratio = jnp.sqrt(grad_sq / cell_count) / jnp.sqrt(prod_sq / cell_count + epsilon)
    scaled = (product * graft_ratio[:, None, None]).astype(jnp.bfloat16)
    returned = lax.all_to_all(
        scaled.reshape(capacity, owners, block_width // owners, quarter),
        "own",
        split_axis=1,
        concat_axis=1,
        tiled=True,
    )
    gathered_back = returned.reshape(capacity * owners, block_width // owners, quarter)
    update = jnp.take(gathered_back, slot_index * owners + owner_list, axis=0)
    return (new_left, new_right, update)


def kernel(
    n_dp,
    n_own,
    owner_ref,
    grads_ref,
    left_stat_ref,
    right_stat_ref,
    left_root_ref,
    right_root_ref,
    new_left_ref,
    new_right_ref,
    update_ref,
    parts,
    summed,
    routed,
    grad,
    left_full,
    right_quarter,
    left_old,
    right_old,
    sent_back,
    came_back,
    norm_sent,
    norm_came,
    ratio_all,
    local_sem,
    sum_send,
    sum_recv,
    root_send,
    root_recv,
    route_send,
    route_recv,
    spread_send,
    spread_recv,
    norm_send,
    norm_recv,
    back_send,
    back_recv,
    ratio_send,
    ratio_recv,
):
    me = lax.axis_index("dp")
    own = lax.axis_index("own")
    blocks, _, rows, width = grads_ref.shape
    capacity, quarter, _ = left_stat_ref.shape
    per_quarter = n_own // n_dp
    dp_of = [lax.rem(me + k, n_dp) for k in range(n_dp)]
    own_of = [lax.rem(own + k, n_own) for k in range(n_own)]

    def to_dp(k, src, dst, send_sem, recv_sem):
        return pltpu.make_async_remote_copy(
            src_ref=src,
            dst_ref=dst,
            send_sem=send_sem,
            recv_sem=recv_sem,
            device_id=(dp_of[k], own),
            device_id_type=MESH,
        )

    def to_own(k, src, dst, send_sem, recv_sem):
        return pltpu.make_async_remote_copy(
            src_ref=src,
            dst_ref=dst,
            send_sem=send_sem,
            recv_sem=recv_sem,
            device_id=(me, own_of[k]),
            device_id_type=MESH,
        )

    local = [
        pltpu.make_async_copy(grads_ref.at[:, me], parts.at[0], local_sem.at[0]),
        pltpu.make_async_copy(right_root_ref, right_quarter, local_sem.at[1]),
        pltpu.make_async_copy(left_stat_ref, left_old, local_sem.at[2]),
        pltpu.make_async_copy(right_stat_ref, right_old, local_sem.at[3]),
    ]
    for k in range(n_dp):
        columns = pl.ds(pl.multiple_of(dp_of[k] * quarter, LANES), quarter)
        local.append(
            pltpu.make_async_copy(
                left_root_ref.at[:, :, columns],
                left_full.at[:, 0, :, pl.ds(k * quarter, quarter)],
                local_sem.at[4 + k],
            )
        )
    for copy in local:
        copy.start()

    barrier = pltpu.get_barrier_semaphore()
    for k in range(1, n_dp):
        pl.semaphore_signal(barrier, inc=1, device_id=(dp_of[k], own), device_id_type=MESH)
    for k in range(1, n_own):
        pl.semaphore_signal(barrier, inc=1, device_id=(me, own_of[k]), device_id_type=MESH)
    pl.semaphore_wait(barrier, n_dp - 1 + n_own - 1)

    sums = [
        to_dp(k, grads_ref.at[:, dp_of[k]], parts.at[k], sum_send.at[k], sum_recv.at[k])
        for k in range(1, n_dp)
    ]
    for copy in sums:
        copy.start()

    named = [owner_ref[b] for b in range(blocks)]
    slot_of = []
    for b in range(blocks):
        before = jnp.int32(0)
        for a in range(b):
            before += (named[a] == named[b]).astype(jnp.int32)
        slot_of.append(jnp.minimum(before, capacity - 1))
    source = {}
    filled = {}
    for k in range(n_own):
        for c in range(capacity):
            source[k, c] = jnp.int32(0)
            filled[k, c] = jnp.int32(0)
            for b in range(blocks):
                hit = jnp.logical_and(named[b] == own_of[k], slot_of[b] == c)
                source[k, c] = jnp.where(hit, jnp.int32(b), source[k, c])
                filled[k, c] = jnp.where(hit, jnp.int32(1), filled[k, c])

    local[0].wait()
    for copy in sums:
        copy.wait_recv()
    total = parts[0].astype(jnp.float32)
    for k in range(1, n_dp):
        total += parts[k].astype(jnp.float32)
    summed[...] = total.astype(jnp.bfloat16)

    def pick(k, c):
        flag = filled[k, c].astype(jnp.float32)
        return (summed[source[k, c]].astype(jnp.float32) * flag).astype(jnp.bfloat16)

    routes = {}
    for k in range(1, n_own):
        for c in range(capacity):
            routed[k, c] = pick(k, c)
        routes[k] = to_own(
            k, routed.at[k], grad.at[:, own, me], route_send.at[k], route_recv.at[k]
        )
        routes[k].start()
    for c in range(capacity):
        grad[c, own, me] = pick(0, c)

    roots = []
    for k in range(1, n_dp):
        at = n_dp - k
        nxt = at % (n_dp - 1) + 1
        for j, column in enumerate((at, nxt)):
            whole = lax.rem(dp_of[k] + column, n_dp)
            columns = pl.ds(pl.multiple_of(whole * quarter, LANES), quarter)
            roots.append(
                to_dp(
                    k,
                    left_root_ref.at[:, :, columns],
                    left_full.at[:, at, :, pl.ds(column * quarter, quarter)],
                    root_send.at[k, j],
                    root_recv.at[k, j],
                )
            )
    for copy in roots:
        copy.start()

    spreads = []
    for k in range(n_own):
        if k:
            routes[k].wait_recv()
        piece = lax.rem(own + n_own - k, n_own)
        for j in range(1, n_dp):
            copy = to_dp(
                j,
                grad.at[:, piece, me],
                grad.at[:, piece, me],
                spread_send.at[k, j],
                spread_recv.at[k, j],
            )
            copy.start()
            spreads.append(copy)

    for copy in local[1:]:
        copy.wait()
    for copy in roots:
        copy.wait_recv()
    for c in range(capacity):
        for k in range(1, n_dp):
            nxt = k % (n_dp - 1) + 1
            left_full[c, k, :, pl.ds(0, quarter)] = left_full[
                c, 0, :, pl.ds(k * quarter, quarter)
            ].T
            left_full[c, nxt, :, pl.ds(k * quarter, quarter)] = left_full[
                c, k, :, pl.ds(nxt * quarter, quarter)
            ].T

    for copy in spreads:
        copy.wait_recv()

    cells = float(width * width)
    nt = (((1,), (1,)), ((), ()))
    tn = (((0,), (0,)), ((), ()))

    def grad_rows(c, k):
        return grad[c, pl.ds(dp_of[k] * per_quarter, per_quarter)].reshape(quarter, width)

    for c in range(capacity):
        half = jnp.concatenate(
            [
                lax.dot_general(
                    grad_rows(c, k), right_quarter[c], nt, preferred_element_type=jnp.float32
                ).astype(jnp.bfloat16)
                for k in range(n_dp)
            ],
            axis=0,
        )
        product = jnp.dot(
            left_full[c].reshape(width, width), half, preferred_element_type=jnp.float32
        )
        for k in range(n_dp):
            piece = product[k * quarter : (k + 1) * quarter].astype(jnp.bfloat16)
            for j in range(per_quarter):
                step = quarter // per_quarter
                sent_back[dp_of[k] * per_quarter + j, c] = piece[j * step : (j + 1) * step]
        norm_sent[c] = jnp.sum(jnp.square(product).reshape(width // 8, 8, quarter), axis=0)
    norms = [
        to_dp(k, norm_sent, norm_came.at[k], norm_send.at[k], norm_recv.at[k])
        for k in range(1, n_dp)
    ]
    for copy in norms:
        copy.start()
    backs = [
        to_own(
            k, sent_back.at[own_of[k]], came_back.at[own], back_send.at[k], back_recv.at[k]
        )
        for k in range(1, n_own)
    ]
    for copy in backs:
        copy.start()
    came_back[own] = sent_back[own]

    grad_sq = []
    for c in range(capacity):
        squares = jnp.square(grad[c].reshape(width, width).astype(jnp.float32))
        grad_sq.append(jnp.sum(squares.reshape(width // 8, 8, width), axis=0))
    for copy in norms:
        copy.wait_recv()
    for c in range(capacity):
        prod_sq = norm_sent[c]
        for k in range(1, n_dp):
            prod_sq += norm_came[k, c]
        prod_all = jnp.sum(prod_sq, keepdims=True).reshape(1, 1)
        grad_all = jnp.sum(grad_sq[c], keepdims=True).reshape(1, 1)
        ratio = jnp.sqrt(grad_all / cells) / jnp.sqrt(prod_all / cells + epsilon)
        ratio_all[own, c] = jnp.broadcast_to(ratio, (8, LANES))
    ratios = [
        to_own(k, ratio_all.at[own], ratio_all.at[own], ratio_send.at[k], ratio_recv.at[k])
        for k in range(1, n_own)
    ]
    for copy in ratios:
        copy.start()

    for c in range(capacity):
        used = filled[0, c].astype(jnp.float32)
        decay = 1.0 - used * (1.0 - decay_rate)
        whole = grad[c].reshape(width, width)
        left_gram = lax.dot_general(
            grad_rows(c, 0), whole, nt, preferred_element_type=jnp.float32
        )
        new_left_ref[c] = decay * left_old[c] + left_gram * (1.0 / width)
        columns = pl.ds(pl.multiple_of(me * quarter, LANES), quarter)
        mine = grad[c, :, :, :, columns].reshape(width, quarter)
        right_gram = lax.dot_general(mine, whole, tn, preferred_element_type=jnp.float32)
        new_right_ref[c] = decay * right_old[c] + right_gram * (1.0 / width)

    for copy in backs:
        copy.wait_recv()
    for copy in ratios:
        copy.wait_recv()
    for b in range(blocks):
        ratio = ratio_all[named[b], slot_of[b]][0:1, :]
        terms = came_back[named[b], slot_of[b]].astype(jnp.float32)
        update_ref[b] = (terms * ratio).astype(jnp.bfloat16)

    for copy in sums + roots + spreads + norms + backs + ratios:
        copy.wait_send()
    for k in routes:
        routes[k].wait_send()


def fused(n_dp, n_own, partial_grads, owner_list, left_stat, right_stat, left_root, right_root):
    capacity, quarter, width = left_stat.shape
    blocks, strip = partial_grads.shape[1:3]
    rows = strip // n_dp
    bf16, f32 = jnp.bfloat16, jnp.float32
    dma = pltpu.SemaphoreType.DMA
    anywhere = pl.BlockSpec(memory_space=pl.ANY)
    return pl.pallas_call(
        functools.partial(kernel, n_dp, n_own),
        out_shape=(
            jax.ShapeDtypeStruct(left_stat.shape, f32),
            jax.ShapeDtypeStruct(right_stat.shape, f32),
            jax.ShapeDtypeStruct((blocks, strip, quarter), bf16),
        ),
        in_specs=[pl.BlockSpec(memory_space=pltpu.SMEM)] + [anywhere] * 5,
        out_specs=tuple([pl.BlockSpec(memory_space=pltpu.VMEM)] * 3),
        scratch_shapes=[
            pltpu.VMEM((n_dp, blocks, rows, width), bf16),
            pltpu.VMEM((blocks, rows, width), bf16),
            pltpu.VMEM((n_own, capacity, rows, width), bf16),
            pltpu.VMEM((capacity, n_own, n_dp, rows, width), bf16),
            pltpu.VMEM((capacity, n_dp, quarter, width), bf16),
            pltpu.VMEM((capacity, quarter, width), bf16),
            pltpu.VMEM((capacity, quarter, width), f32),
            pltpu.VMEM((capacity, quarter, width), f32),
            pltpu.VMEM((n_own, capacity, strip, quarter), bf16),
            pltpu.VMEM((n_own, capacity, strip, quarter), bf16),
            pltpu.VMEM((capacity, 8, LANES), f32),
            pltpu.VMEM((n_dp, capacity, 8, LANES), f32),
            pltpu.VMEM((n_own, capacity, 8, LANES), f32),
            dma((4 + n_dp,)),
            dma((n_dp,)),
            dma((n_dp,)),
            dma((n_dp, 2)),
            dma((n_dp, 2)),
            dma((n_own,)),
            dma((n_own,)),
            dma((n_own, n_dp)),
            dma((n_own, n_dp)),
            dma((n_dp,)),
            dma((n_dp,)),
            dma((n_own,)),
            dma((n_own,)),
            dma((n_own,)),
            dma((n_own,)),
        ],
        compiler_params=pltpu.CompilerParams(
            collective_id=0, has_side_effects=True, vmem_limit_bytes=40 * 1024 * 1024
        ),
    )(
        owner_list,
        partial_grads[0].reshape(blocks, n_dp, rows, width),
        left_stat,
        right_stat,
        left_root,
        right_root,
    )


def solution(mesh):
    n_dp, n_own = mesh.shape["dp"], mesh.shape["own"]
    in_specs = (
        P("dp", None, "own", None),
        P(),
        P("own", "dp", None),
        P("own", "dp", None),
        P("own", "dp", None),
        P("own", "dp", None),
    )
    out_specs = (P("own", "dp", None), P("own", "dp", None), P(None, "own", "dp"))

    def step(*operands):
        strip = operands[0].shape[2]
        quarter = operands[2].shape[1]
        fits = (
            n_dp == 4
            and n_own % n_dp == 0
            and strip % (16 * n_dp) == 0
            and quarter == LANES
            and strip * n_own == quarter * n_dp
        )
        if fits:
            return fused(n_dp, n_own, *operands)
        return body(*operands)

    return jax.shard_map(step, mesh=mesh, in_specs=in_specs, out_specs=out_specs, check_vma=False)
```

```python
import functools

import jax
import jax.numpy as jnp
from jax import lax
from jax.experimental import pallas as pl
from jax.experimental.pallas import tpu as pltpu
from jax.sharding import PartitionSpec as P

decay_rate = 0.95
epsilon = 1e-06

MESH = pl.DeviceIdType.MESH
LANES = 128


def body(partial_grads, owner_list, left_stat, right_stat, left_root, right_root):
    owners = lax.axis_size("own")
    capacity = left_stat.shape[0]
    quarter = left_stat.shape[1]
    block_width = left_stat.shape[2]
    blocks = owner_list.shape[0]
    owner_hits = (owner_list[:, None] == jnp.arange(owners, dtype=jnp.int32)[None, :]).astype(
        jnp.int32
    )
    before = jnp.cumsum(owner_hits, axis=0) - owner_hits
    slot_index = jnp.sum(before * owner_hits, axis=1)
    slot_hits = (slot_index[:, None] == jnp.arange(capacity, dtype=jnp.int32)[None, :]).astype(
        jnp.int32
    )
    slot_match = slot_hits[:, :, None] * owner_hits[:, None, :]
    source_block = jnp.sum(slot_match * jnp.arange(blocks, dtype=jnp.int32)[:, None, None], axis=0)
    filled_flag = jnp.sum(slot_match, axis=0).astype(jnp.bfloat16)
    local_terms = partial_grads[0].astype(jnp.float32)
    shared = lax.psum(local_terms.astype(jnp.bfloat16), "dp")
    outgoing = jnp.take(shared, source_block, axis=0) * filled_flag[:, :, None, None]
    arrived = lax.all_to_all(outgoing, "own", split_axis=1, concat_axis=1, tiled=True)
    grad_part = arrived.reshape(capacity, block_width, arrived.shape[3])
    dp_lane = lax.axis_index("dp")
    own_index = lax.axis_index("own")
    owner_load = jnp.sum((owner_list == own_index).astype(jnp.int32))
    slot_used = (jnp.arange(capacity, dtype=jnp.int32) < owner_load)[:, None, None]
    row_start = dp_lane * quarter
    grad_rows = lax.dynamic_slice_in_dim(grad_part, row_start, quarter, 1)
    grad_colq = lax.dynamic_slice_in_dim(grad_part, row_start, quarter, 2)
    left_gram = jnp.einsum("cqk,cnk->cqn", grad_rows, grad_part, preferred_element_type=jnp.float32)
    right_gram = jnp.einsum(
        "ckq,ckn->cqn", grad_colq, grad_part, preferred_element_type=jnp.float32
    )
    new_left = jnp.where(slot_used, decay_rate * left_stat + left_gram / block_width, left_stat)
    new_right = jnp.where(slot_used, decay_rate * right_stat + right_gram / block_width, right_stat)
    half_done = jnp.einsum(
        "ckn,cqn->ckq", grad_part, right_root, preferred_element_type=jnp.float32
    ).astype(jnp.bfloat16)
    product = jnp.einsum(
        "cpn,cpq->cnq",
        lax.all_gather(left_root, "dp", axis=1, tiled=True),
        half_done,
        preferred_element_type=jnp.float32,
    )
    grad_sq = jnp.sum(jnp.square(grad_part.astype(jnp.float32)), axis=(1, 2))
    prod_sq = lax.psum(jnp.sum(product * product, axis=(1, 2)), "dp")
    cell_count = float(block_width * block_width)
    graft_ratio = jnp.sqrt(grad_sq / cell_count) / jnp.sqrt(prod_sq / cell_count + epsilon)
    scaled = (product * graft_ratio[:, None, None]).astype(jnp.bfloat16)
    returned = lax.all_to_all(
        scaled.reshape(capacity, owners, block_width // owners, quarter),
        "own",
        split_axis=1,
        concat_axis=1,
        tiled=True,
    )
    gathered_back = returned.reshape(capacity * owners, block_width // owners, quarter)
    update = jnp.take(gathered_back, slot_index * owners + owner_list, axis=0)
    return (new_left, new_right, update)


def kernel(
    n_dp,
    n_own,
    owner_ref,
    grads_ref,
    left_stat_ref,
    right_stat_ref,
    left_root_ref,
    right_root_ref,
    new_left_ref,
    new_right_ref,
    update_ref,
    parts,
    summed,
    routed,
    grad,
    left_full,
    right_quarter,
    left_old,
    right_old,
    sent_back,
    came_back,
    norm_sent,
    norm_came,
    ratio_all,
    local_sem,
    sum_send,
    sum_recv,
    root_send,
    root_recv,
    route_send,
    route_recv,
    spread_send,
    spread_recv,
    norm_send,
    norm_recv,
    back_send,
    back_recv,
    ratio_send,
    ratio_recv,
):
    me = lax.axis_index("dp")
    own = lax.axis_index("own")
    blocks, _, rows, width = grads_ref.shape
    capacity, quarter, _ = left_stat_ref.shape
    per_quarter = n_own // n_dp
    dp_of = [lax.rem(me + k, n_dp) for k in range(n_dp)]
    own_of = [lax.rem(own + k, n_own) for k in range(n_own)]

    def to_dp(k, src, dst, send_sem, recv_sem):
        return pltpu.make_async_remote_copy(
            src_ref=src,
            dst_ref=dst,
            send_sem=send_sem,
            recv_sem=recv_sem,
            device_id=(dp_of[k], own),
            device_id_type=MESH,
        )

    def to_own(k, src, dst, send_sem, recv_sem):
        return pltpu.make_async_remote_copy(
            src_ref=src,
            dst_ref=dst,
            send_sem=send_sem,
            recv_sem=recv_sem,
            device_id=(me, own_of[k]),
            device_id_type=MESH,
        )

    local = [
        pltpu.make_async_copy(grads_ref.at[:, me], parts.at[0], local_sem.at[0]),
        pltpu.make_async_copy(right_root_ref, right_quarter, local_sem.at[1]),
        pltpu.make_async_copy(left_stat_ref, left_old, local_sem.at[2]),
        pltpu.make_async_copy(right_stat_ref, right_old, local_sem.at[3]),
    ]
    for k in range(n_dp):
        columns = pl.ds(pl.multiple_of(dp_of[k] * quarter, LANES), quarter)
        local.append(
            pltpu.make_async_copy(
                left_root_ref.at[:, :, columns],
                left_full.at[:, 0, :, pl.ds(k * quarter, quarter)],
                local_sem.at[4 + k],
            )
        )
    for copy in local:
        copy.start()

    barrier = pltpu.get_barrier_semaphore()
    for k in range(1, n_dp):
        pl.semaphore_signal(barrier, inc=1, device_id=(dp_of[k], own), device_id_type=MESH)
    for k in range(1, n_own):
        pl.semaphore_signal(barrier, inc=1, device_id=(me, own_of[k]), device_id_type=MESH)
    pl.semaphore_wait(barrier, n_dp - 1 + n_own - 1)

    sums = [
        to_dp(k, grads_ref.at[:, dp_of[k]], parts.at[k], sum_send.at[k], sum_recv.at[k])
        for k in range(1, n_dp)
    ]
    for copy in sums:
        copy.start()

    roots = []
    for j in range(2):
        for k in range(1, n_dp):
            at = n_dp - k
            column = (at, at % (n_dp - 1) + 1)[j]
            whole = lax.rem(dp_of[k] + column, n_dp)
            columns = pl.ds(pl.multiple_of(whole * quarter, LANES), quarter)
            roots.append(
                to_dp(
                    k,
                    left_root_ref.at[:, :, columns],
                    left_full.at[:, at, :, pl.ds(column * quarter, quarter)],
                    root_send.at[k, j],
                    root_recv.at[k, j],
                )
            )
    for copy in roots[: n_dp - 1]:
        copy.start()

    named = [owner_ref[b] for b in range(blocks)]
    slot_of = []
    for b in range(blocks):
        before = jnp.int32(0)
        for a in range(b):
            before += (named[a] == named[b]).astype(jnp.int32)
        slot_of.append(jnp.minimum(before, capacity - 1))
    source = {}
    filled = {}
    for k in range(n_own):
        for c in range(capacity):
            source[k, c] = jnp.int32(0)
            filled[k, c] = jnp.int32(0)
            for b in range(blocks):
                hit = jnp.logical_and(named[b] == own_of[k], slot_of[b] == c)
                source[k, c] = jnp.where(hit, jnp.int32(b), source[k, c])
                filled[k, c] = jnp.where(hit, jnp.int32(1), filled[k, c])

    local[0].wait()
    for copy in sums:
        copy.wait_recv()
    total = parts[0].astype(jnp.float32)
    for k in range(1, n_dp):
        total += parts[k].astype(jnp.float32)
    summed[...] = total.astype(jnp.bfloat16)

    def pick(k, c):
        flag = filled[k, c].astype(jnp.float32)
        return (summed[source[k, c]].astype(jnp.float32) * flag).astype(jnp.bfloat16)

    routes = {}
    for c in range(capacity):
        for k in range(1, n_own):
            routed[k, c] = pick(k, c)
            routes[c, k] = to_own(
                k,
                routed.at[k, c],
                grad.at[c, own, me],
                route_send.at[c, k],
                route_recv.at[c, k],
            )
            routes[c, k].start()
        grad[c, own, me] = pick(0, c)
    for copy in roots[n_dp - 1 :]:
        copy.start()

    spreads = {}
    for c in range(capacity):
        for k in range(n_own):
            if k:
                routes[c, k].wait_recv()
            piece = lax.rem(own + n_own - k, n_own)
            for j in range(1, n_dp):
                copy = to_dp(
                    j,
                    grad.at[c, piece, me],
                    grad.at[c, piece, me],
                    spread_send.at[c, k, j],
                    spread_recv.at[c, k, j],
                )
                copy.start()
                spreads[c, k, j] = copy

    for copy in local[1:]:
        copy.wait()
    for copy in roots:
        copy.wait_recv()
    for c in range(capacity):
        for k in range(1, n_dp):
            nxt = k % (n_dp - 1) + 1
            left_full[c, k, :, pl.ds(0, quarter)] = left_full[
                c, 0, :, pl.ds(k * quarter, quarter)
            ].T
            left_full[c, nxt, :, pl.ds(k * quarter, quarter)] = left_full[
                c, k, :, pl.ds(nxt * quarter, quarter)
            ].T

    cells = float(width * width)
    nt = (((1,), (1,)), ((), ()))
    tn = (((0,), (0,)), ((), ()))

    def grad_rows(c, k):
        return grad[c, pl.ds(dp_of[k] * per_quarter, per_quarter)].reshape(quarter, width)

    norms = {}
    backs = {}
    ratios = {}
    for c in range(capacity):
        for k in range(n_own):
            for j in range(1, n_dp):
                spreads[c, k, j].wait_recv()
        half = jnp.concatenate(
            [
                lax.dot_general(
                    grad_rows(c, k), right_quarter[c], nt, preferred_element_type=jnp.float32
                ).astype(jnp.bfloat16)
                for k in range(n_dp)
            ],
            axis=0,
        )
        product = jnp.dot(
            left_full[c].reshape(width, width), half, preferred_element_type=jnp.float32
        )
        for k in range(n_dp):
            piece = product[k * quarter : (k + 1) * quarter].astype(jnp.bfloat16)
            for j in range(per_quarter):
                step = quarter // per_quarter
                sent_back[c, dp_of[k] * per_quarter + j] = piece[j * step : (j + 1) * step]
        norm_sent[c] = jnp.sum(jnp.square(product).reshape(width // 8, 8, quarter), axis=0)
        for k in range(1, n_dp):
            norms[c, k] = to_dp(
                k, norm_sent.at[c], norm_came.at[c, k], norm_send.at[c, k], norm_recv.at[c, k]
            )
            norms[c, k].start()
        for k in range(1, n_own):
            backs[c, k] = to_own(
                k,
                sent_back.at[c, own_of[k]],
                came_back.at[c, own],
                back_send.at[c, k],
                back_recv.at[c, k],
            )
            backs[c, k].start()
        came_back[c, own] = sent_back[c, own]

    for c in range(capacity):
        squares = jnp.square(grad[c].reshape(width, width).astype(jnp.float32))
        grad_sq = jnp.sum(squares.reshape(width // 8, 8, width), axis=0)
        prod_sq = norm_sent[c]
        for k in range(1, n_dp):
            norms[c, k].wait_recv()
            prod_sq += norm_came[c, k]
        prod_all = jnp.sum(prod_sq, keepdims=True).reshape(1, 1)
        grad_all = jnp.sum(grad_sq, keepdims=True).reshape(1, 1)
        ratio = jnp.sqrt(grad_all / cells) / jnp.sqrt(prod_all / cells + epsilon)
        ratio_all[own, c] = jnp.broadcast_to(ratio, (8, LANES))
    for k in range(1, n_own):
        ratios[k] = to_own(
            k, ratio_all.at[own], ratio_all.at[own], ratio_send.at[k], ratio_recv.at[k]
        )
        ratios[k].start()

    for c in range(capacity):
        used = filled[0, c].astype(jnp.float32)
        decay = 1.0 - used * (1.0 - decay_rate)
        whole = grad[c].reshape(width, width)
        left_gram = lax.dot_general(
            grad_rows(c, 0), whole, nt, preferred_element_type=jnp.float32
        )
        new_left_ref[c] = decay * left_old[c] + left_gram * (1.0 / width)
        columns = pl.ds(pl.multiple_of(me * quarter, LANES), quarter)
        mine = grad[c, :, :, :, columns].reshape(width, quarter)
        right_gram = lax.dot_general(mine, whole, tn, preferred_element_type=jnp.float32)
        new_right_ref[c] = decay * right_old[c] + right_gram * (1.0 / width)

    for copy in [*backs.values(), *ratios.values()]:
        copy.wait_recv()
    for b in range(blocks):
        ratio = ratio_all[named[b], slot_of[b]][0:1, :]
        terms = came_back[slot_of[b], named[b]].astype(jnp.float32)
        update_ref[b] = (terms * ratio).astype(jnp.bfloat16)

    for copy in sums + roots:
        copy.wait_send()
    for group in (routes, spreads, norms, backs, ratios):
        for copy in group.values():
            copy.wait_send()


def fused(n_dp, n_own, partial_grads, owner_list, left_stat, right_stat, left_root, right_root):
    capacity, quarter, width = left_stat.shape
    blocks, strip = partial_grads.shape[1:3]
    rows = strip // n_dp
    bf16, f32 = jnp.bfloat16, jnp.float32
    dma = pltpu.SemaphoreType.DMA
    anywhere = pl.BlockSpec(memory_space=pltpu.HBM)
    return pl.pallas_call(
        functools.partial(kernel, n_dp, n_own),
        out_shape=(
            jax.ShapeDtypeStruct(left_stat.shape, f32),
            jax.ShapeDtypeStruct(right_stat.shape, f32),
            jax.ShapeDtypeStruct((blocks, strip, quarter), bf16),
        ),
        in_specs=[pl.BlockSpec(memory_space=pltpu.SMEM)] + [anywhere] * 5,
        out_specs=tuple([pl.BlockSpec(memory_space=pltpu.VMEM)] * 3),
        scratch_shapes=[
            pltpu.VMEM((n_dp, blocks, rows, width), bf16),
            pltpu.VMEM((blocks, rows, width), bf16),
            pltpu.VMEM((n_own, capacity, rows, width), bf16),
            pltpu.VMEM((capacity, n_own, n_dp, rows, width), bf16),
            pltpu.VMEM((capacity, n_dp, quarter, width), bf16),
            pltpu.VMEM((capacity, quarter, width), bf16),
            pltpu.VMEM((capacity, quarter, width), f32),
            pltpu.VMEM((capacity, quarter, width), f32),
            pltpu.VMEM((capacity, n_own, strip, quarter), bf16),
            pltpu.VMEM((capacity, n_own, strip, quarter), bf16),
            pltpu.VMEM((capacity, 8, LANES), f32),
            pltpu.VMEM((capacity, n_dp, 8, LANES), f32),
            pltpu.VMEM((n_own, capacity, 8, LANES), f32),
            dma((4 + n_dp,)),
            dma((n_dp,)),
            dma((n_dp,)),
            dma((n_dp, 2)),
            dma((n_dp, 2)),
            dma((capacity, n_own)),
            dma((capacity, n_own)),
            dma((capacity, n_own, n_dp)),
            dma((capacity, n_own, n_dp)),
            dma((capacity, n_dp)),
            dma((capacity, n_dp)),
            dma((capacity, n_own)),
            dma((capacity, n_own)),
            dma((n_own,)),
            dma((n_own,)),
        ],
        compiler_params=pltpu.CompilerParams(
            collective_id=0, has_side_effects=True, vmem_limit_bytes=62 * 1024 * 1024
        ),
    )(
        owner_list,
        partial_grads[0].reshape(blocks, n_dp, rows, width),
        left_stat,
        right_stat,
        left_root,
        right_root,
    )


def solution(mesh):
    n_dp, n_own = mesh.shape["dp"], mesh.shape["own"]
    in_specs = (
        P("dp", None, "own", None),
        P(),
        P("own", "dp", None),
        P("own", "dp", None),
        P("own", "dp", None),
        P("own", "dp", None),
    )
    out_specs = (P("own", "dp", None), P("own", "dp", None), P(None, "own", "dp"))

    def step(*operands):
        strip = operands[0].shape[2]
        quarter = operands[2].shape[1]
        fits = (
            n_dp == 4
            and n_own % n_dp == 0
            and strip % (16 * n_dp) == 0
            and quarter == LANES
            and strip * n_own == quarter * n_dp
        )
        if fits:
            return fused(n_dp, n_own, *operands)
        return body(*operands)

    return jax.shard_map(step, mesh=mesh, in_specs=in_specs, out_specs=out_specs, check_vma=False)
```

```python
import functools

import jax
import jax.numpy as jnp
from jax import lax
from jax.experimental import pallas as pl
from jax.experimental.pallas import tpu as pltpu
from jax.sharding import PartitionSpec as P

decay_rate = 0.95
epsilon = 1e-06

MESH = pl.DeviceIdType.MESH
LANES = 128


def body(partial_grads, owner_list, left_stat, right_stat, left_root, right_root):
    owners = lax.axis_size("own")
    capacity = left_stat.shape[0]
    quarter = left_stat.shape[1]
    block_width = left_stat.shape[2]
    blocks = owner_list.shape[0]
    owner_hits = (owner_list[:, None] == jnp.arange(owners, dtype=jnp.int32)[None, :]).astype(
        jnp.int32
    )
    before = jnp.cumsum(owner_hits, axis=0) - owner_hits
    slot_index = jnp.sum(before * owner_hits, axis=1)
    slot_hits = (slot_index[:, None] == jnp.arange(capacity, dtype=jnp.int32)[None, :]).astype(
        jnp.int32
    )
    slot_match = slot_hits[:, :, None] * owner_hits[:, None, :]
    source_block = jnp.sum(slot_match * jnp.arange(blocks, dtype=jnp.int32)[:, None, None], axis=0)
    filled_flag = jnp.sum(slot_match, axis=0).astype(jnp.bfloat16)
    local_terms = partial_grads[0].astype(jnp.float32)
    shared = lax.psum(local_terms.astype(jnp.bfloat16), "dp")
    outgoing = jnp.take(shared, source_block, axis=0) * filled_flag[:, :, None, None]
    arrived = lax.all_to_all(outgoing, "own", split_axis=1, concat_axis=1, tiled=True)
    grad_part = arrived.reshape(capacity, block_width, arrived.shape[3])
    dp_lane = lax.axis_index("dp")
    own_index = lax.axis_index("own")
    owner_load = jnp.sum((owner_list == own_index).astype(jnp.int32))
    slot_used = (jnp.arange(capacity, dtype=jnp.int32) < owner_load)[:, None, None]
    row_start = dp_lane * quarter
    grad_rows = lax.dynamic_slice_in_dim(grad_part, row_start, quarter, 1)
    grad_colq = lax.dynamic_slice_in_dim(grad_part, row_start, quarter, 2)
    left_gram = jnp.einsum("cqk,cnk->cqn", grad_rows, grad_part, preferred_element_type=jnp.float32)
    right_gram = jnp.einsum(
        "ckq,ckn->cqn", grad_colq, grad_part, preferred_element_type=jnp.float32
    )
    new_left = jnp.where(slot_used, decay_rate * left_stat + left_gram / block_width, left_stat)
    new_right = jnp.where(slot_used, decay_rate * right_stat + right_gram / block_width, right_stat)
    half_done = jnp.einsum(
        "ckn,cqn->ckq", grad_part, right_root, preferred_element_type=jnp.float32
    ).astype(jnp.bfloat16)
    product = jnp.einsum(
        "cpn,cpq->cnq",
        lax.all_gather(left_root, "dp", axis=1, tiled=True),
        half_done,
        preferred_element_type=jnp.float32,
    )
    grad_sq = jnp.sum(jnp.square(grad_part.astype(jnp.float32)), axis=(1, 2))
    prod_sq = lax.psum(jnp.sum(product * product, axis=(1, 2)), "dp")
    cell_count = float(block_width * block_width)
    graft_ratio = jnp.sqrt(grad_sq / cell_count) / jnp.sqrt(prod_sq / cell_count + epsilon)
    scaled = (product * graft_ratio[:, None, None]).astype(jnp.bfloat16)
    returned = lax.all_to_all(
        scaled.reshape(capacity, owners, block_width // owners, quarter),
        "own",
        split_axis=1,
        concat_axis=1,
        tiled=True,
    )
    gathered_back = returned.reshape(capacity * owners, block_width // owners, quarter)
    update = jnp.take(gathered_back, slot_index * owners + owner_list, axis=0)
    return (new_left, new_right, update)


def kernel(
    n_dp,
    n_own,
    owner_ref,
    grads_ref,
    left_stat_ref,
    right_stat_ref,
    left_root_ref,
    right_root_ref,
    new_left_ref,
    new_right_ref,
    update_ref,
    parts,
    summed,
    routed,
    grad,
    left_full,
    right_quarter,
    left_old,
    right_old,
    sent_back,
    came_back,
    norm_sent,
    norm_came,
    ratio_all,
    local_sem,
    sum_send,
    sum_recv,
    root_send,
    root_recv,
    route_send,
    route_recv,
    spread_send,
    spread_recv,
    norm_send,
    norm_recv,
    back_send,
    back_recv,
    ratio_send,
    ratio_recv,
):
    me = lax.axis_index("dp")
    own = lax.axis_index("own")
    blocks, _, rows, width = grads_ref.shape
    capacity, quarter, _ = left_stat_ref.shape
    per_quarter = n_own // n_dp
    dp_of = [me, me + 1 - 2 * (me % 2), me + 2 - 4 * (me // 2), 3 - me]
    own_of = [lax.rem(own + k, n_own) for k in range(n_own)]

    def to_dp(k, src, dst, send_sem, recv_sem):
        return pltpu.make_async_remote_copy(
            src_ref=src,
            dst_ref=dst,
            send_sem=send_sem,
            recv_sem=recv_sem,
            device_id=(dp_of[k], own),
            device_id_type=MESH,
        )

    def to_own(k, src, dst, send_sem, recv_sem):
        return pltpu.make_async_remote_copy(
            src_ref=src,
            dst_ref=dst,
            send_sem=send_sem,
            recv_sem=recv_sem,
            device_id=(me, own_of[k]),
            device_id_type=MESH,
        )

    local = [
        pltpu.make_async_copy(grads_ref.at[:, me], parts.at[0], local_sem.at[0]),
        pltpu.make_async_copy(right_root_ref, right_quarter, local_sem.at[1]),
        pltpu.make_async_copy(left_stat_ref, left_old, local_sem.at[2]),
        pltpu.make_async_copy(right_stat_ref, right_old, local_sem.at[3]),
    ]
    for k in range(n_dp):
        columns = pl.ds(pl.multiple_of(dp_of[k] * quarter, LANES), quarter)
        local.append(
            pltpu.make_async_copy(
                left_root_ref.at[:, :, columns],
                left_full.at[:, 0, :, pl.ds(k * quarter, quarter)],
                local_sem.at[4 + k],
            )
        )
    for copy in local:
        copy.start()

    barrier = pltpu.get_barrier_semaphore()
    for k in range(1, n_dp):
        pl.semaphore_signal(barrier, inc=1, device_id=(dp_of[k], own), device_id_type=MESH)
    for k in range(1, n_own):
        pl.semaphore_signal(barrier, inc=1, device_id=(me, own_of[k]), device_id_type=MESH)
    pl.semaphore_wait(barrier, n_dp - 1 + n_own - 1)

    sums = [
        to_dp(k, grads_ref.at[:, dp_of[k]], parts.at[k], sum_send.at[k], sum_recv.at[k])
        for k in range(1, n_dp)
    ]
    for copy in sums:
        copy.start()

    roots = []
    for j in range(2):
        for k in range(1, n_dp):
            column = (k, k % (n_dp - 1) + 1)[j]
            columns = pl.ds(pl.multiple_of(dp_of[k ^ column] * quarter, LANES), quarter)
            roots.append(
                to_dp(
                    k,
                    left_root_ref.at[:, :, columns],
                    left_full.at[:, k, :, pl.ds(column * quarter, quarter)],
                    root_send.at[k, j],
                    root_recv.at[k, j],
                )
            )
    for copy in roots[: n_dp - 1]:
        copy.start()

    named = [owner_ref[b] for b in range(blocks)]
    slot_of = []
    for b in range(blocks):
        before = jnp.int32(0)
        for a in range(b):
            before += (named[a] == named[b]).astype(jnp.int32)
        slot_of.append(jnp.minimum(before, capacity - 1))
    source = {}
    filled = {}
    for k in range(n_own):
        for c in range(capacity):
            source[k, c] = jnp.int32(0)
            filled[k, c] = jnp.int32(0)
            for b in range(blocks):
                hit = jnp.logical_and(named[b] == own_of[k], slot_of[b] == c)
                source[k, c] = jnp.where(hit, jnp.int32(b), source[k, c])
                filled[k, c] = jnp.where(hit, jnp.int32(1), filled[k, c])

    local[0].wait()
    for copy in sums:
        copy.wait_recv()
    total = parts[0].astype(jnp.float32)
    for k in range(1, n_dp):
        total += parts[k].astype(jnp.float32)
    summed[...] = total.astype(jnp.bfloat16)

    def pick(k, c):
        flag = filled[k, c].astype(jnp.float32)
        return (summed[source[k, c]].astype(jnp.float32) * flag).astype(jnp.bfloat16)

    routes = {}
    for c in range(capacity):
        for k in range(1, n_own):
            routed[k, c] = pick(k, c)
            routes[c, k] = to_own(
                k,
                routed.at[k, c],
                grad.at[c, own, me],
                route_send.at[c, k],
                route_recv.at[c, k],
            )
            routes[c, k].start()
        grad[c, own, me] = pick(0, c)
    for copy in roots[n_dp - 1 :]:
        copy.start()

    spreads = {}
    arrived = set()

    def spread(c, k, j, source_at):
        piece = lax.rem(own + n_own - k, n_own)
        across = 3 if source_at else j
        spreads[c, k, across] = to_dp(
            j,
            grad.at[c, piece, dp_of[source_at]],
            grad.at[c, piece, dp_of[source_at]],
            spread_send.at[c, k, across],
            spread_recv.at[c, k, across],
        )
        spreads[c, k, across].start()

    def relay(c, k):
        came = 1 + (c + k) % 2
        spreads[c, k, came].wait_recv()
        arrived.add((c, k, came))
        spread(c, k, 3 - came, came)

    lag = 3
    order = [(c, k) for c in range(capacity) for k in range(n_own)]
    for at, (c, k) in enumerate(order):
        if k:
            routes[c, k].wait_recv()
        spread(c, k, 1, 0)
        spread(c, k, 2, 0)
        if at >= lag:
            relay(*order[at - lag])
    for c, k in order[-lag:]:
        relay(c, k)

    for copy in local[1:]:
        copy.wait()
    for copy in roots:
        copy.wait_recv()
    for c in range(capacity):
        for k in range(1, n_dp):
            nxt = k % (n_dp - 1) + 1
            left_full[c, k, :, pl.ds(0, quarter)] = left_full[
                c, 0, :, pl.ds(k * quarter, quarter)
            ].T
            left_full[c, nxt, :, pl.ds(k * quarter, quarter)] = left_full[
                c, k, :, pl.ds(nxt * quarter, quarter)
            ].T

    cells = float(width * width)
    nt = (((1,), (1,)), ((), ()))
    tn = (((0,), (0,)), ((), ()))

    def grad_rows(c, k):
        return grad[c, pl.ds(dp_of[k] * per_quarter, per_quarter)].reshape(quarter, width)

    norms = {}
    backs = {}
    ratios = {}
    for c in range(capacity):
        for k in range(n_own):
            for j in range(1, n_dp):
                if (c, k, j) not in arrived:
                    spreads[c, k, j].wait_recv()
        half = jnp.concatenate(
            [
                lax.dot_general(
                    grad_rows(c, k), right_quarter[c], nt, preferred_element_type=jnp.float32
                ).astype(jnp.bfloat16)
                for k in range(n_dp)
            ],
            axis=0,
        )
        product = jnp.dot(
            left_full[c].reshape(width, width), half, preferred_element_type=jnp.float32
        )
        for k in range(n_dp):
            piece = product[k * quarter : (k + 1) * quarter].astype(jnp.bfloat16)
            for j in range(per_quarter):
                step = quarter // per_quarter
                sent_back[c, dp_of[k] * per_quarter + j] = piece[j * step : (j + 1) * step]
        norm_sent[c] = jnp.sum(jnp.square(product).reshape(width // 8, 8, quarter), axis=0)
        for k in range(1, n_dp):
            norms[c, k] = to_dp(
                k, norm_sent.at[c], norm_came.at[c, k], norm_send.at[c, k], norm_recv.at[c, k]
            )
            norms[c, k].start()
        for k in range(1, n_own):
            backs[c, k] = to_own(
                k,
                sent_back.at[c, own_of[k]],
                came_back.at[c, own],
                back_send.at[c, k],
                back_recv.at[c, k],
            )
            backs[c, k].start()
        came_back[c, own] = sent_back[c, own]

    for c in range(capacity):
        squares = jnp.square(grad[c].reshape(width, width).astype(jnp.float32))
        grad_sq = jnp.sum(squares.reshape(width // 8, 8, width), axis=0)
        prod_sq = norm_sent[c]
        for k in range(1, n_dp):
            norms[c, k].wait_recv()
            prod_sq += norm_came[c, k]
        prod_all = jnp.sum(prod_sq, keepdims=True).reshape(1, 1)
        grad_all = jnp.sum(grad_sq, keepdims=True).reshape(1, 1)
        ratio = jnp.sqrt(grad_all / cells) / jnp.sqrt(prod_all / cells + epsilon)
        ratio_all[own, c] = jnp.broadcast_to(ratio, (8, LANES))
    for k in range(1, n_own):
        ratios[k] = to_own(
            k, ratio_all.at[own], ratio_all.at[own], ratio_send.at[k], ratio_recv.at[k]
        )
        ratios[k].start()

    for c in range(capacity):
        used = filled[0, c].astype(jnp.float32)
        decay = 1.0 - used * (1.0 - decay_rate)
        whole = grad[c].reshape(width, width)
        left_gram = lax.dot_general(
            grad_rows(c, 0), whole, nt, preferred_element_type=jnp.float32
        )
        new_left_ref[c] = decay * left_old[c] + left_gram * (1.0 / width)
        columns = pl.ds(pl.multiple_of(me * quarter, LANES), quarter)
        mine = grad[c, :, :, :, columns].reshape(width, quarter)
        right_gram = lax.dot_general(mine, whole, tn, preferred_element_type=jnp.float32)
        new_right_ref[c] = decay * right_old[c] + right_gram * (1.0 / width)

    for copy in [*backs.values(), *ratios.values()]:
        copy.wait_recv()
    for b in range(blocks):
        ratio = ratio_all[named[b], slot_of[b]][0:1, :]
        terms = came_back[slot_of[b], named[b]].astype(jnp.float32)
        update_ref[b] = (terms * ratio).astype(jnp.bfloat16)

    for copy in sums + roots:
        copy.wait_send()
    for group in (routes, spreads, norms, backs, ratios):
        for copy in group.values():
            copy.wait_send()


def write_out(*refs):
    inputs, outputs, sems = refs[:3], refs[3:6], refs[6]
    copies = [
        pltpu.make_async_copy(inputs[i], outputs[i], sems.at[i]) for i in range(len(inputs))
    ]
    for copy in copies:
        copy.start()
    for copy in copies:
        copy.wait()


def fused(n_dp, n_own, partial_grads, owner_list, left_stat, right_stat, left_root, right_root):
    capacity, quarter, width = left_stat.shape
    blocks, strip = partial_grads.shape[1:3]
    rows = strip // n_dp
    bf16, f32 = jnp.bfloat16, jnp.float32
    dma = pltpu.SemaphoreType.DMA
    anywhere = pl.BlockSpec(memory_space=pltpu.HBM)
    hbm = functools.partial(pltpu.with_memory_space_constraint, memory_space=pltpu.HBM)
    shapes = (left_stat.shape, right_stat.shape, (blocks, strip, quarter))
    types = (f32, f32, bf16)
    results = pl.pallas_call(
        functools.partial(kernel, n_dp, n_own),
        out_shape=tuple(pltpu.VMEM(shape, kind) for shape, kind in zip(shapes, types)),
        in_specs=[pl.BlockSpec(memory_space=pltpu.SMEM)] + [anywhere] * 5,
        out_specs=tuple([pl.BlockSpec(memory_space=pltpu.VMEM)] * 3),
        scratch_shapes=[
            pltpu.VMEM((n_dp, blocks, rows, width), bf16),
            pltpu.VMEM((blocks, rows, width), bf16),
            pltpu.VMEM((n_own, capacity, rows, width), bf16),
            pltpu.VMEM((capacity, n_own, n_dp, rows, width), bf16),
            pltpu.VMEM((capacity, n_dp, quarter, width), bf16),
            pltpu.VMEM((capacity, quarter, width), bf16),
            pltpu.VMEM((capacity, quarter, width), f32),
            pltpu.VMEM((capacity, quarter, width), f32),
            pltpu.VMEM((capacity, n_own, strip, quarter), bf16),
            pltpu.VMEM((capacity, n_own, strip, quarter), bf16),
            pltpu.VMEM((capacity, 8, LANES), f32),
            pltpu.VMEM((capacity, n_dp, 8, LANES), f32),
            pltpu.VMEM((n_own, capacity, 8, LANES), f32),
            dma((4 + n_dp,)),
            dma((n_dp,)),
            dma((n_dp,)),
            dma((n_dp, 2)),
            dma((n_dp, 2)),
            dma((capacity, n_own)),
            dma((capacity, n_own)),
            dma((capacity, n_own, n_dp)),
            dma((capacity, n_own, n_dp)),
            dma((capacity, n_dp)),
            dma((capacity, n_dp)),
            dma((capacity, n_own)),
            dma((capacity, n_own)),
            dma((n_own,)),
            dma((n_own,)),
        ],
        compiler_params=pltpu.CompilerParams(
            collective_id=0, has_side_effects=True, vmem_limit_bytes=40 * 1024 * 1024
        ),
    )(
        hbm(owner_list),
        hbm(partial_grads[0].reshape(blocks, n_dp, rows, width)),
        hbm(left_stat),
        hbm(right_stat),
        hbm(left_root),
        hbm(right_root),
    )
    return pl.pallas_call(
        write_out,
        out_shape=tuple(jax.ShapeDtypeStruct(shape, kind) for shape, kind in zip(shapes, types)),
        in_specs=[pl.BlockSpec(memory_space=pltpu.VMEM)] * 3,
        out_specs=tuple([pl.BlockSpec(memory_space=pltpu.HBM)] * 3),
        scratch_shapes=[dma((3,))],
    )(*results)


def solution(mesh):
    n_dp, n_own = mesh.shape["dp"], mesh.shape["own"]
    in_specs = (
        P("dp", None, "own", None),
        P(),
        P("own", "dp", None),
        P("own", "dp", None),
        P("own", "dp", None),
        P("own", "dp", None),
    )
    out_specs = (P("own", "dp", None), P("own", "dp", None), P(None, "own", "dp"))

    def step(*operands):
        strip = operands[0].shape[2]
        quarter = operands[2].shape[1]
        fits = (
            n_dp == 4
            and n_own % n_dp == 0
            and strip % (16 * n_dp) == 0
            and quarter == LANES
            and strip * n_own == quarter * n_dp
        )
        if fits:
            return fused(n_dp, n_own, *operands)
        return body(*operands)

    return jax.shard_map(step, mesh=mesh, in_specs=in_specs, out_specs=out_specs, check_vma=False)
```

```python
import functools

import jax
import jax.numpy as jnp
from jax import lax
from jax.experimental import pallas as pl
from jax.experimental.pallas import tpu as pltpu
from jax.sharding import PartitionSpec as P

decay_rate = 0.95
epsilon = 1e-06

MESH = pl.DeviceIdType.MESH
LANES = 128


def body(partial_grads, owner_list, left_stat, right_stat, left_root, right_root):
    owners = lax.axis_size("own")
    capacity = left_stat.shape[0]
    quarter = left_stat.shape[1]
    block_width = left_stat.shape[2]
    blocks = owner_list.shape[0]
    owner_hits = (owner_list[:, None] == jnp.arange(owners, dtype=jnp.int32)[None, :]).astype(
        jnp.int32
    )
    before = jnp.cumsum(owner_hits, axis=0) - owner_hits
    slot_index = jnp.sum(before * owner_hits, axis=1)
    slot_hits = (slot_index[:, None] == jnp.arange(capacity, dtype=jnp.int32)[None, :]).astype(
        jnp.int32
    )
    slot_match = slot_hits[:, :, None] * owner_hits[:, None, :]
    source_block = jnp.sum(slot_match * jnp.arange(blocks, dtype=jnp.int32)[:, None, None], axis=0)
    filled_flag = jnp.sum(slot_match, axis=0).astype(jnp.bfloat16)
    local_terms = partial_grads[0].astype(jnp.float32)
    shared = lax.psum(local_terms.astype(jnp.bfloat16), "dp")
    outgoing = jnp.take(shared, source_block, axis=0) * filled_flag[:, :, None, None]
    arrived = lax.all_to_all(outgoing, "own", split_axis=1, concat_axis=1, tiled=True)
    grad_part = arrived.reshape(capacity, block_width, arrived.shape[3])
    dp_lane = lax.axis_index("dp")
    own_index = lax.axis_index("own")
    owner_load = jnp.sum((owner_list == own_index).astype(jnp.int32))
    slot_used = (jnp.arange(capacity, dtype=jnp.int32) < owner_load)[:, None, None]
    row_start = dp_lane * quarter
    grad_rows = lax.dynamic_slice_in_dim(grad_part, row_start, quarter, 1)
    grad_colq = lax.dynamic_slice_in_dim(grad_part, row_start, quarter, 2)
    left_gram = jnp.einsum("cqk,cnk->cqn", grad_rows, grad_part, preferred_element_type=jnp.float32)
    right_gram = jnp.einsum(
        "ckq,ckn->cqn", grad_colq, grad_part, preferred_element_type=jnp.float32
    )
    new_left = jnp.where(slot_used, decay_rate * left_stat + left_gram / block_width, left_stat)
    new_right = jnp.where(slot_used, decay_rate * right_stat + right_gram / block_width, right_stat)
    half_done = jnp.einsum(
        "ckn,cqn->ckq", grad_part, right_root, preferred_element_type=jnp.float32
    ).astype(jnp.bfloat16)
    product = jnp.einsum(
        "cpn,cpq->cnq",
        lax.all_gather(left_root, "dp", axis=1, tiled=True),
        half_done,
        preferred_element_type=jnp.float32,
    )
    grad_sq = jnp.sum(jnp.square(grad_part.astype(jnp.float32)), axis=(1, 2))
    prod_sq = lax.psum(jnp.sum(product * product, axis=(1, 2)), "dp")
    cell_count = float(block_width * block_width)
    graft_ratio = jnp.sqrt(grad_sq / cell_count) / jnp.sqrt(prod_sq / cell_count + epsilon)
    scaled = (product * graft_ratio[:, None, None]).astype(jnp.bfloat16)
    returned = lax.all_to_all(
        scaled.reshape(capacity, owners, block_width // owners, quarter),
        "own",
        split_axis=1,
        concat_axis=1,
        tiled=True,
    )
    gathered_back = returned.reshape(capacity * owners, block_width // owners, quarter)
    update = jnp.take(gathered_back, slot_index * owners + owner_list, axis=0)
    return (new_left, new_right, update)


def kernel(
    n_dp,
    n_own,
    owner_ref,
    grads_ref,
    left_stat_ref,
    right_stat_ref,
    left_root_ref,
    right_root_ref,
    new_left_ref,
    new_right_ref,
    update_ref,
    parts,
    summed,
    routed,
    grad,
    left_full,
    right_quarter,
    left_old,
    right_old,
    sent_back,
    came_back,
    norm_sent,
    norm_came,
    ratio_all,
    local_sem,
    send_sem,
    recv_sem,
):
    me = lax.axis_index("dp")
    own = lax.axis_index("own")
    blocks, _, rows, width = grads_ref.shape
    capacity, quarter, _ = left_stat_ref.shape
    per_quarter = n_own // n_dp
    dp_of = [me, me + 1 - 2 * (me % 2), me + 2 - 4 * (me // 2), 3 - me]
    own_of = [lax.rem(own + k, n_own) for k in range(n_own)]

    def send(src, dst, group, c, device):
        pltpu.make_async_remote_copy(
            src_ref=src,
            dst_ref=dst,
            send_sem=send_sem.at[group, c],
            recv_sem=recv_sem.at[group, c],
            device_id=device,
            device_id_type=MESH,
        ).start()

    def to_dp(k, src, dst, group, c):
        send(src, dst, group, c, (dp_of[k], own))

    def to_own(k, src, dst, group, c):
        send(src, dst, group, c, (me, own_of[k]))

    def wait_for(sem, like):
        pltpu.make_async_copy(like, like, sem).wait()

    sums, roots, routes, spreads, norms, backs, ratios = range(7)
    sizes = {
        sums: parts.at[pl.ds(1, n_dp - 1)],
        roots: left_full.at[:, pl.ds(1, n_dp - 1), :, pl.ds(0, 2 * quarter)],
        routes: grad.at[0, pl.ds(1, n_own - 1), 0],
        spreads: grad.at[0, :, pl.ds(1, n_dp - 1)],
        norms: norm_came.at[0, pl.ds(1, n_dp - 1)],
        backs: came_back.at[0, pl.ds(1, n_own - 1)],
        ratios: ratio_all.at[pl.ds(1, n_own - 1)],
    }

    def arrived(group, c=0):
        wait_for(recv_sem.at[group, c], sizes[group])

    local = [
        pltpu.make_async_copy(grads_ref.at[:, me], parts.at[0], local_sem.at[0]),
        pltpu.make_async_copy(right_root_ref, right_quarter, local_sem.at[1]),
        pltpu.make_async_copy(left_stat_ref, left_old, local_sem.at[2]),
        pltpu.make_async_copy(right_stat_ref, right_old, local_sem.at[3]),
    ]
    for k in range(n_dp):
        columns = pl.ds(pl.multiple_of(dp_of[k] * quarter, LANES), quarter)
        local.append(
            pltpu.make_async_copy(
                left_root_ref.at[:, :, columns],
                left_full.at[:, 0, :, pl.ds(k * quarter, quarter)],
                local_sem.at[4 + k],
            )
        )
    for copy in local:
        copy.start()

    barrier = pltpu.get_barrier_semaphore()
    for k in range(1, n_dp):
        pl.semaphore_signal(barrier, inc=1, device_id=(dp_of[k], own), device_id_type=MESH)
    for k in range(1, n_own):
        pl.semaphore_signal(barrier, inc=1, device_id=(me, own_of[k]), device_id_type=MESH)
    pl.semaphore_wait(barrier, n_dp - 1 + n_own - 1)

    for k in range(1, n_dp):
        to_dp(k, grads_ref.at[:, dp_of[k]], parts.at[k], sums, 0)

    named = [owner_ref[b] for b in range(blocks)]
    slot_of = []
    for b in range(blocks):
        before = jnp.int32(0)
        for a in range(b):
            before += (named[a] == named[b]).astype(jnp.int32)
        slot_of.append(jnp.minimum(before, capacity - 1))
    source = {}
    filled = {}
    for k in range(n_own):
        for c in range(capacity):
            source[k, c] = jnp.int32(0)
            filled[k, c] = jnp.int32(0)
            for b in range(blocks):
                hit = jnp.logical_and(named[b] == own_of[k], slot_of[b] == c)
                source[k, c] = jnp.where(hit, jnp.int32(b), source[k, c])
                filled[k, c] = jnp.where(hit, jnp.int32(1), filled[k, c])

    local[0].wait()
    arrived(sums)
    total = parts[0].astype(jnp.float32)
    for k in range(1, n_dp):
        total += parts[k].astype(jnp.float32)
    summed[...] = total.astype(jnp.bfloat16)

    def pick(k, c):
        flag = filled[k, c].astype(jnp.float32)
        return (summed[source[k, c]].astype(jnp.float32) * flag).astype(jnp.bfloat16)

    for c in range(capacity):
        for k in range(1, n_own):
            routed[k, c] = pick(k, c)
            to_own(k, routed.at[k, c], grad.at[c, own, me], routes, c)
        grad[c, own, me] = pick(0, c)

    for k in range(1, n_dp):
        for column in (k, k % (n_dp - 1) + 1):
            columns = pl.ds(pl.multiple_of(dp_of[k ^ column] * quarter, LANES), quarter)
            to_dp(
                k,
                left_root_ref.at[:, :, columns],
                left_full.at[:, k, :, pl.ds(column * quarter, quarter)],
                roots,
                0,
            )

    for c in range(capacity):
        arrived(routes, c)
        for k in range(1, n_dp):
            to_dp(k, grad.at[c, :, me], grad.at[c, :, me], spreads, c)

    for copy in local[1:]:
        copy.wait()
    arrived(roots)
    for c in range(capacity):
        for k in range(1, n_dp):
            nxt = k % (n_dp - 1) + 1
            left_full[c, k, :, pl.ds(0, quarter)] = left_full[
                c, 0, :, pl.ds(k * quarter, quarter)
            ].T
            left_full[c, nxt, :, pl.ds(k * quarter, quarter)] = left_full[
                c, k, :, pl.ds(nxt * quarter, quarter)
            ].T

    cells = float(width * width)
    nt = (((1,), (1,)), ((), ()))
    tn = (((0,), (0,)), ((), ()))

    def grad_rows(c, k):
        return grad[c, pl.ds(dp_of[k] * per_quarter, per_quarter)].reshape(quarter, width)

    def statistics(c):
        used = filled[0, c].astype(jnp.float32)
        decay = 1.0 - used * (1.0 - decay_rate)
        whole = grad[c].reshape(width, width)
        left_gram = lax.dot_general(
            grad_rows(c, 0), whole, nt, preferred_element_type=jnp.float32
        )
        new_left_ref[c] = decay * left_old[c] + left_gram * (1.0 / width)
        columns = pl.ds(pl.multiple_of(me * quarter, LANES), quarter)
        mine = grad[c, :, :, :, columns].reshape(width, quarter)
        right_gram = lax.dot_general(mine, whole, tn, preferred_element_type=jnp.float32)
        new_right_ref[c] = decay * right_old[c] + right_gram * (1.0 / width)

    for c in range(capacity):
        arrived(spreads, c)
        half = jnp.concatenate(
            [
                lax.dot_general(
                    grad_rows(c, k), right_quarter[c], nt, preferred_element_type=jnp.float32
                ).astype(jnp.bfloat16)
                for k in range(n_dp)
            ],
            axis=0,
        )
        product = jnp.dot(
            left_full[c].reshape(width, width), half, preferred_element_type=jnp.float32
        )
        for k in range(n_dp):
            piece = product[k * quarter : (k + 1) * quarter].astype(jnp.bfloat16)
            for j in range(per_quarter):
                step = quarter // per_quarter
                sent_back[c, dp_of[k] * per_quarter + j] = piece[j * step : (j + 1) * step]
        norm_sent[c] = jnp.sum(jnp.square(product).reshape(width // 8, 8, quarter), axis=0)
        for k in range(1, n_dp):
            to_dp(k, norm_sent.at[c], norm_came.at[c, k], norms, c)
        for k in range(1, n_own):
            to_own(k, sent_back.at[c, own_of[k]], came_back.at[c, own], backs, c)
        came_back[c, own] = sent_back[c, own]
        if c < capacity - 1:
            statistics(c)

    for c in range(capacity):
        squares = jnp.square(grad[c].reshape(width, width).astype(jnp.float32))
        grad_sq = jnp.sum(squares.reshape(width // 8, 8, width), axis=0)
        arrived(norms, c)
        prod_sq = norm_sent[c]
        for k in range(1, n_dp):
            prod_sq += norm_came[c, k]
        prod_all = jnp.sum(prod_sq, keepdims=True).reshape(1, 1)
        grad_all = jnp.sum(grad_sq, keepdims=True).reshape(1, 1)
        ratio = jnp.sqrt(grad_all / cells) / jnp.sqrt(prod_all / cells + epsilon)
        ratio_all[own, c] = jnp.broadcast_to(ratio, (8, LANES))
    for k in range(1, n_own):
        to_own(k, ratio_all.at[own], ratio_all.at[own], ratios, 0)
    statistics(capacity - 1)

    for c in range(capacity):
        arrived(backs, c)
    arrived(ratios)
    for b in range(blocks):
        ratio = ratio_all[named[b], slot_of[b]][0:1, :]
        terms = came_back[slot_of[b], named[b]].astype(jnp.float32)
        update_ref[b] = (terms * ratio).astype(jnp.bfloat16)

    for group in sizes:
        for c in range(1 if group in (sums, roots, ratios) else capacity):
            wait_for(send_sem.at[group, c], sizes[group])


def write_out(*refs):
    inputs, outputs, sems = refs[:3], refs[3:6], refs[6]
    copies = [
        pltpu.make_async_copy(inputs[i], outputs[i], sems.at[i]) for i in range(len(inputs))
    ]
    for copy in copies:
        copy.start()
    for copy in copies:
        copy.wait()


def fused(n_dp, n_own, partial_grads, owner_list, left_stat, right_stat, left_root, right_root):
    capacity, quarter, width = left_stat.shape
    blocks, strip = partial_grads.shape[1:3]
    rows = strip // n_dp
    bf16, f32 = jnp.bfloat16, jnp.float32
    dma = pltpu.SemaphoreType.DMA
    anywhere = pl.BlockSpec(memory_space=pl.ANY)
    hbm = functools.partial(pltpu.with_memory_space_constraint, memory_space=pltpu.HBM)
    shapes = (left_stat.shape, right_stat.shape, (blocks, strip, quarter))
    types = (f32, f32, bf16)
    results = pl.pallas_call(
        functools.partial(kernel, n_dp, n_own),
        out_shape=tuple(pltpu.VMEM(shape, kind) for shape, kind in zip(shapes, types)),
        in_specs=[pl.BlockSpec(memory_space=pltpu.SMEM)] + [anywhere] * 5,
        out_specs=tuple([pl.BlockSpec(memory_space=pltpu.VMEM)] * 3),
        scratch_shapes=[
            pltpu.VMEM((n_dp, blocks, rows, width), bf16),
            pltpu.VMEM((blocks, rows, width), bf16),
            pltpu.VMEM((n_own, capacity, rows, width), bf16),
            pltpu.VMEM((capacity, n_own, n_dp, rows, width), bf16),
            pltpu.VMEM((capacity, n_dp, quarter, width), bf16),
            pltpu.VMEM((capacity, quarter, width), bf16),
            pltpu.VMEM((capacity, quarter, width), f32),
            pltpu.VMEM((capacity, quarter, width), f32),
            pltpu.VMEM((capacity, n_own, strip, quarter), bf16),
            pltpu.VMEM((capacity, n_own, strip, quarter), bf16),
            pltpu.VMEM((capacity, 8, LANES), f32),
            pltpu.VMEM((capacity, n_dp, 8, LANES), f32),
            pltpu.VMEM((n_own, capacity, 8, LANES), f32),
            dma((4 + n_dp,)),
            dma((7, capacity)),
            dma((7, capacity)),
        ],
        compiler_params=pltpu.CompilerParams(
            collective_id=0, has_side_effects=True, vmem_limit_bytes=40 * 1024 * 1024
        ),
    )(
        hbm(owner_list),
        hbm(partial_grads[0].reshape(blocks, n_dp, rows, width)),
        hbm(left_stat),
        hbm(right_stat),
        hbm(left_root),
        hbm(right_root),
    )
    return pl.pallas_call(
        write_out,
        out_shape=tuple(jax.ShapeDtypeStruct(shape, kind) for shape, kind in zip(shapes, types)),
        in_specs=[anywhere] * 3,
        out_specs=tuple([pl.BlockSpec(memory_space=pltpu.HBM)] * 3),
        scratch_shapes=[dma((3,))],
        compiler_params=pltpu.CompilerParams(vmem_limit_bytes=4 * 1024 * 1024),
    )(*[pltpu.with_memory_space_constraint(x, pltpu.VMEM) for x in results])


def solution(mesh):
    n_dp, n_own = mesh.shape["dp"], mesh.shape["own"]
    in_specs = (
        P("dp", None, "own", None),
        P(),
        P("own", "dp", None),
        P("own", "dp", None),
        P("own", "dp", None),
        P("own", "dp", None),
    )
    out_specs = (P("own", "dp", None), P("own", "dp", None), P(None, "own", "dp"))

    def step(*operands):
        strip = operands[0].shape[2]
        quarter = operands[2].shape[1]
        fits = (
            n_dp == 4
            and n_own % n_dp == 0
            and strip % (16 * n_dp) == 0
            and quarter == LANES
            and strip * n_own == quarter * n_dp
        )
        if fits:
            return fused(n_dp, n_own, *operands)
        return body(*operands)

    return jax.shard_map(step, mesh=mesh, in_specs=in_specs, out_specs=out_specs, check_vma=False)
```

```python
import functools

import jax
import jax.numpy as jnp
from jax import lax
from jax.experimental import pallas as pl
from jax.experimental.pallas import tpu as pltpu
from jax.sharding import PartitionSpec as P

decay_rate = 0.95
epsilon = 1e-06

MESH = pl.DeviceIdType.MESH
LANES = 128


def body(partial_grads, owner_list, left_stat, right_stat, left_root, right_root):
    owners = lax.axis_size("own")
    capacity = left_stat.shape[0]
    quarter = left_stat.shape[1]
    block_width = left_stat.shape[2]
    blocks = owner_list.shape[0]
    owner_hits = (owner_list[:, None] == jnp.arange(owners, dtype=jnp.int32)[None, :]).astype(
        jnp.int32
    )
    before = jnp.cumsum(owner_hits, axis=0) - owner_hits
    slot_index = jnp.sum(before * owner_hits, axis=1)
    slot_hits = (slot_index[:, None] == jnp.arange(capacity, dtype=jnp.int32)[None, :]).astype(
        jnp.int32
    )
    slot_match = slot_hits[:, :, None] * owner_hits[:, None, :]
    source_block = jnp.sum(slot_match * jnp.arange(blocks, dtype=jnp.int32)[:, None, None], axis=0)
    filled_flag = jnp.sum(slot_match, axis=0).astype(jnp.bfloat16)
    local_terms = partial_grads[0].astype(jnp.float32)
    shared = lax.psum(local_terms.astype(jnp.bfloat16), "dp")
    outgoing = jnp.take(shared, source_block, axis=0) * filled_flag[:, :, None, None]
    arrived = lax.all_to_all(outgoing, "own", split_axis=1, concat_axis=1, tiled=True)
    grad_part = arrived.reshape(capacity, block_width, arrived.shape[3])
    dp_lane = lax.axis_index("dp")
    own_index = lax.axis_index("own")
    owner_load = jnp.sum((owner_list == own_index).astype(jnp.int32))
    slot_used = (jnp.arange(capacity, dtype=jnp.int32) < owner_load)[:, None, None]
    row_start = dp_lane * quarter
    grad_rows = lax.dynamic_slice_in_dim(grad_part, row_start, quarter, 1)
    grad_colq = lax.dynamic_slice_in_dim(grad_part, row_start, quarter, 2)
    left_gram = jnp.einsum("cqk,cnk->cqn", grad_rows, grad_part, preferred_element_type=jnp.float32)
    right_gram = jnp.einsum(
        "ckq,ckn->cqn", grad_colq, grad_part, preferred_element_type=jnp.float32
    )
    new_left = jnp.where(slot_used, decay_rate * left_stat + left_gram / block_width, left_stat)
    new_right = jnp.where(slot_used, decay_rate * right_stat + right_gram / block_width, right_stat)
    half_done = jnp.einsum(
        "ckn,cqn->ckq", grad_part, right_root, preferred_element_type=jnp.float32
    ).astype(jnp.bfloat16)
    product = jnp.einsum(
        "cpn,cpq->cnq",
        lax.all_gather(left_root, "dp", axis=1, tiled=True),
        half_done,
        preferred_element_type=jnp.float32,
    )
    grad_sq = jnp.sum(jnp.square(grad_part.astype(jnp.float32)), axis=(1, 2))
    prod_sq = lax.psum(jnp.sum(product * product, axis=(1, 2)), "dp")
    cell_count = float(block_width * block_width)
    graft_ratio = jnp.sqrt(grad_sq / cell_count) / jnp.sqrt(prod_sq / cell_count + epsilon)
    scaled = (product * graft_ratio[:, None, None]).astype(jnp.bfloat16)
    returned = lax.all_to_all(
        scaled.reshape(capacity, owners, block_width // owners, quarter),
        "own",
        split_axis=1,
        concat_axis=1,
        tiled=True,
    )
    gathered_back = returned.reshape(capacity * owners, block_width // owners, quarter)
    update = jnp.take(gathered_back, slot_index * owners + owner_list, axis=0)
    return (new_left, new_right, update)


def kernel(
    n_dp,
    n_own,
    owner_ref,
    grads_ref,
    left_stat_ref,
    right_stat_ref,
    left_root_ref,
    right_root_ref,
    new_left_ref,
    new_right_ref,
    update_ref,
    parts,
    summed,
    routed,
    grad,
    left_full,
    right_quarter,
    left_old,
    right_old,
    sent_back,
    came_back,
    norm_sent,
    norm_came,
    ratio_all,
    local_sem,
    send_sem,
    recv_sem,
    spread_send,
    spread_recv,
):
    me = lax.axis_index("dp")
    own = lax.axis_index("own")
    blocks, _, rows, width = grads_ref.shape
    capacity, quarter, _ = left_stat_ref.shape
    per_quarter = n_own // n_dp
    dp_of = [me, me + 1 - 2 * (me % 2), me + 2 - 4 * (me // 2), 3 - me]
    near = n_own // 2
    base = (own // near) * near
    turn = own - base
    own_of = [base + lax.rem(turn + k, near) for k in range(near)]
    own_of += [near - base + lax.rem(turn + k, near) for k in range(near)]

    def send(src, dst, group, c, device):
        pltpu.make_async_remote_copy(
            src_ref=src,
            dst_ref=dst,
            send_sem=send_sem.at[group, c],
            recv_sem=recv_sem.at[group, c],
            device_id=device,
            device_id_type=MESH,
        ).start()

    def to_dp(k, src, dst, group, c):
        send(src, dst, group, c, (dp_of[k], own))

    def to_own(k, src, dst, group, c):
        send(src, dst, group, c, (me, own_of[k]))

    def wait_for(sem, like):
        pltpu.make_async_copy(like, like, sem).wait()

    sums, roots, routes_near, routes_far, norms, backs, ratios = range(7)
    sizes = {
        sums: parts.at[pl.ds(1, n_dp - 1)],
        roots: left_full.at[:, pl.ds(1, n_dp - 1), :, pl.ds(0, 2 * quarter)],
        routes_near: grad.at[0, pl.ds(1, near - 1), 0],
        routes_far: grad.at[0, pl.ds(0, near), 0],
        norms: norm_came.at[0, pl.ds(1, n_dp - 1)],
        backs: came_back.at[0, pl.ds(1, n_own - 1)],
        ratios: ratio_all.at[pl.ds(1, n_own - 1)],
    }

    def arrived(group, c=0):
        wait_for(recv_sem.at[group, c], sizes[group])

    local = [
        pltpu.make_async_copy(grads_ref.at[:, me], parts.at[0], local_sem.at[0]),
        pltpu.make_async_copy(right_root_ref, right_quarter, local_sem.at[1]),
        pltpu.make_async_copy(left_stat_ref, left_old, local_sem.at[2]),
        pltpu.make_async_copy(right_stat_ref, right_old, local_sem.at[3]),
    ]
    for k in range(n_dp):
        columns = pl.ds(pl.multiple_of(dp_of[k] * quarter, LANES), quarter)
        local.append(
            pltpu.make_async_copy(
                left_root_ref.at[:, :, columns],
                left_full.at[:, 0, :, pl.ds(k * quarter, quarter)],
                local_sem.at[4 + k],
            )
        )
    for copy in local:
        copy.start()

    barrier = pltpu.get_barrier_semaphore()
    for k in range(1, n_dp):
        pl.semaphore_signal(barrier, inc=1, device_id=(dp_of[k], own), device_id_type=MESH)
    for k in range(1, n_own):
        pl.semaphore_signal(barrier, inc=1, device_id=(me, own_of[k]), device_id_type=MESH)
    pl.semaphore_wait(barrier, n_dp - 1 + n_own - 1)

    for k in range(1, n_dp):
        to_dp(k, grads_ref.at[:, dp_of[k]], parts.at[k], sums, 0)

    def send_root(k, column, slots):
        columns = pl.ds(pl.multiple_of(dp_of[k ^ column] * quarter, LANES), quarter)
        to_dp(
            k,
            left_root_ref.at[slots, :, columns],
            left_full.at[slots, k, :, pl.ds(column * quarter, quarter)],
            roots,
            0,
        )

    every = pl.ds(0, capacity)
    root_pieces = [(1, 1, every), (2, 2, every), (3, 3, every), (1, 3, every), (2, 3, every)]
    root_pieces += [(1 + c % 2, 2 - c % 2, pl.ds(c, 1)) for c in range(capacity)]
    for copy in root_pieces[: n_dp - 1]:
        send_root(*copy)

    named = [owner_ref[b] for b in range(blocks)]
    slot_of = []
    for b in range(blocks):
        before = jnp.int32(0)
        for a in range(b):
            before += (named[a] == named[b]).astype(jnp.int32)
        slot_of.append(jnp.minimum(before, capacity - 1))
    source = {}
    filled = {}
    for k in range(n_own):
        for c in range(capacity):
            source[k, c] = jnp.int32(0)
            filled[k, c] = jnp.int32(0)
            for b in range(blocks):
                hit = jnp.logical_and(named[b] == own_of[k], slot_of[b] == c)
                source[k, c] = jnp.where(hit, jnp.int32(b), source[k, c])
                filled[k, c] = jnp.where(hit, jnp.int32(1), filled[k, c])

    local[0].wait()
    arrived(sums)
    total = parts[0].astype(jnp.float32)
    for k in range(1, n_dp):
        total += parts[k].astype(jnp.float32)
    summed[...] = total.astype(jnp.bfloat16)

    def pick(k, c):
        flag = filled[k, c].astype(jnp.float32)
        return (summed[source[k, c]].astype(jnp.float32) * flag).astype(jnp.bfloat16)

    for c in range(capacity):
        for k in range(1, n_own):
            routed[k, c] = pick(k, c)
            group = routes_near if k < near else routes_far
            to_own(k, routed.at[k, c], grad.at[c, own, me], group, c)
        grad[c, own, me] = pick(0, c)

    for copy in root_pieces[n_dp - 1 :]:
        send_root(*copy)

    def half_of(c, far, at):
        start = near - base if far else base
        return grad.at[c, pl.ds(start, near), dp_of[at]]

    def spread(c, far, k, at):
        piece = half_of(c, far, at)
        across = k ^ at
        pltpu.make_async_remote_copy(
            src_ref=piece,
            dst_ref=piece,
            send_sem=spread_send.at[c, far, across],
            recv_sem=spread_recv.at[c, far, across],
            device_id=(dp_of[k], own),
            device_id_type=MESH,
        ).start()

    def spread_arrived(c, far, at):
        wait_for(spread_recv.at[c, far, at], half_of(c, far, at))

    def start_spread(c, far):
        arrived(routes_far if far else routes_near, c)
        for k in (2, 1) if far else (1, 2):
            spread(c, far, k, 0)

    def relay(c, far):
        came = 2 if far else 1
        spread_arrived(c, far, came)
        spread(c, far, 3 - came, came)

    halves = [(c, far) for c in range(capacity) for far in range(2)]
    lag = 2
    for at, half in enumerate(halves):
        start_spread(*half)
        if at >= lag:
            relay(*halves[at - lag])

    for copy in local[1:]:
        copy.wait()
    arrived(roots)
    for c in range(capacity):
        for i, j in ((0, 1), (0, 2), (0, 3), (1, 3), (2, 3), (1 + c % 2, 2 - c % 2)):
            left_full[c, j, :, pl.ds(i * quarter, quarter)] = left_full[
                c, i, :, pl.ds(j * quarter, quarter)
            ].T
    for half in halves[-lag:]:
        relay(*half)

    cells = float(width * width)
    nt = (((1,), (1,)), ((), ()))
    tn = (((0,), (0,)), ((), ()))

    def grad_rows(c, k):
        return grad[c, pl.ds(dp_of[k] * per_quarter, per_quarter)].reshape(quarter, width)

    def statistics(c):
        used = filled[0, c].astype(jnp.float32)
        decay = 1.0 - used * (1.0 - decay_rate)
        whole = grad[c].reshape(width, width)
        left_gram = lax.dot_general(
            grad_rows(c, 0), whole, nt, preferred_element_type=jnp.float32
        )
        new_left_ref[c] = decay * left_old[c] + left_gram * (1.0 / width)
        columns = pl.ds(pl.multiple_of(me * quarter, LANES), quarter)
        mine = grad[c, :, :, :, columns].reshape(width, quarter)
        right_gram = lax.dot_general(mine, whole, tn, preferred_element_type=jnp.float32)
        new_right_ref[c] = decay * right_old[c] + right_gram * (1.0 / width)

    for c in range(capacity):
        for far in range(2):
            spread_arrived(c, far, 1 if far else 2)
            spread_arrived(c, far, 3)
        half = jnp.concatenate(
            [
                lax.dot_general(
                    grad_rows(c, k), right_quarter[c], nt, preferred_element_type=jnp.float32
                ).astype(jnp.bfloat16)
                for k in range(n_dp)
            ],
            axis=0,
        )
        product = jnp.dot(
            left_full[c].reshape(width, width), half, preferred_element_type=jnp.float32
        )
        for k in range(n_dp):
            piece = product[k * quarter : (k + 1) * quarter].astype(jnp.bfloat16)
            for j in range(per_quarter):
                step = quarter // per_quarter
                sent_back[c, dp_of[k] * per_quarter + j] = piece[j * step : (j + 1) * step]
        norm_sent[c] = jnp.sum(jnp.square(product).reshape(width // 8, 8, quarter), axis=0)
        for k in range(1, n_dp):
            to_dp(k, norm_sent.at[c], norm_came.at[c, k], norms, c)
        for k in reversed(range(1, n_own)):
            to_own(k, sent_back.at[c, own_of[k]], came_back.at[c, own], backs, c)
        came_back[c, own] = sent_back[c, own]

    for c in range(capacity):
        squares = jnp.square(grad[c].reshape(width, width).astype(jnp.float32))
        grad_sq = jnp.sum(squares.reshape(width // 8, 8, width), axis=0)
        arrived(norms, c)
        prod_sq = norm_sent[c]
        for k in range(1, n_dp):
            prod_sq += norm_came[c, k]
        prod_all = jnp.sum(prod_sq, keepdims=True).reshape(1, 1)
        grad_all = jnp.sum(grad_sq, keepdims=True).reshape(1, 1)
        ratio = jnp.sqrt(grad_all / cells) / jnp.sqrt(prod_all / cells + epsilon)
        ratio_all[own, c] = jnp.broadcast_to(ratio, (8, LANES))
    for k in range(1, n_own):
        to_own(k, ratio_all.at[own], ratio_all.at[own], ratios, 0)
    for c in range(capacity):
        statistics(c)

    for c in range(capacity):
        arrived(backs, c)
    arrived(ratios)
    for b in range(blocks):
        ratio = ratio_all[named[b], slot_of[b]][0:1, :]
        terms = came_back[slot_of[b], named[b]].astype(jnp.float32)
        update_ref[b] = (terms * ratio).astype(jnp.bfloat16)

    for group in sizes:
        for c in range(1 if group in (sums, roots, ratios) else capacity):
            wait_for(send_sem.at[group, c], sizes[group])
    for c, far in halves:
        for k in range(1, n_dp):
            wait_for(spread_send.at[c, far, k], half_of(c, far, 0))


def write_out(*refs):
    inputs, outputs, sems = refs[:3], refs[3:6], refs[6]
    copies = [
        pltpu.make_async_copy(inputs[i], outputs[i], sems.at[i]) for i in range(len(inputs))
    ]
    for copy in copies:
        copy.start()
    for copy in copies:
        copy.wait()


def fused(n_dp, n_own, partial_grads, owner_list, left_stat, right_stat, left_root, right_root):
    capacity, quarter, width = left_stat.shape
    blocks, strip = partial_grads.shape[1:3]
    rows = strip // n_dp
    bf16, f32 = jnp.bfloat16, jnp.float32
    dma = pltpu.SemaphoreType.DMA
    anywhere = pl.BlockSpec(memory_space=pl.ANY)
    hbm = functools.partial(pltpu.with_memory_space_constraint, memory_space=pltpu.HBM)
    shapes = (left_stat.shape, right_stat.shape, (blocks, strip, quarter))
    types = (f32, f32, bf16)
    results = pl.pallas_call(
        functools.partial(kernel, n_dp, n_own),
        out_shape=tuple(pltpu.VMEM(shape, kind) for shape, kind in zip(shapes, types)),
        in_specs=[pl.BlockSpec(memory_space=pltpu.SMEM)] + [anywhere] * 5,
        out_specs=tuple([pl.BlockSpec(memory_space=pltpu.VMEM)] * 3),
        scratch_shapes=[
            pltpu.VMEM((n_dp, blocks, rows, width), bf16),
            pltpu.VMEM((blocks, rows, width), bf16),
            pltpu.VMEM((n_own, capacity, rows, width), bf16),
            pltpu.VMEM((capacity, n_own, n_dp, rows, width), bf16),
            pltpu.VMEM((capacity, n_dp, quarter, width), bf16),
            pltpu.VMEM((capacity, quarter, width), bf16),
            pltpu.VMEM((capacity, quarter, width), f32),
            pltpu.VMEM((capacity, quarter, width), f32),
            pltpu.VMEM((capacity, n_own, strip, quarter), bf16),
            pltpu.VMEM((capacity, n_own, strip, quarter), bf16),
            pltpu.VMEM((capacity, 8, LANES), f32),
            pltpu.VMEM((capacity, n_dp, 8, LANES), f32),
            pltpu.VMEM((n_own, capacity, 8, LANES), f32),
            dma((4 + n_dp,)),
            dma((7, capacity)),
            dma((7, capacity)),
            dma((capacity, 2, n_dp)),
            dma((capacity, 2, n_dp)),
        ],
        compiler_params=pltpu.CompilerParams(
            collective_id=0, has_side_effects=True, vmem_limit_bytes=40 * 1024 * 1024
        ),
    )(
        hbm(owner_list),
        hbm(partial_grads[0].reshape(blocks, n_dp, rows, width)),
        hbm(left_stat),
        hbm(right_stat),
        hbm(left_root),
        hbm(right_root),
    )
    return pl.pallas_call(
        write_out,
        out_shape=tuple(jax.ShapeDtypeStruct(shape, kind) for shape, kind in zip(shapes, types)),
        in_specs=[anywhere] * 3,
        out_specs=tuple([pl.BlockSpec(memory_space=pltpu.HBM)] * 3),
        scratch_shapes=[dma((3,))],
        compiler_params=pltpu.CompilerParams(vmem_limit_bytes=4 * 1024 * 1024),
    )(*[pltpu.with_memory_space_constraint(x, pltpu.VMEM) for x in results])


def solution(mesh):
    n_dp, n_own = mesh.shape["dp"], mesh.shape["own"]
    in_specs = (
        P("dp", None, "own", None),
        P(),
        P("own", "dp", None),
        P("own", "dp", None),
        P("own", "dp", None),
        P("own", "dp", None),
    )
    out_specs = (P("own", "dp", None), P("own", "dp", None), P(None, "own", "dp"))

    def step(*operands):
        strip = operands[0].shape[2]
        quarter = operands[2].shape[1]
        fits = (
            n_dp == 4
            and n_own % n_dp == 0
            and n_own >= 2 * n_dp
            and strip % (16 * n_dp) == 0
            and quarter == LANES
            and strip * n_own == quarter * n_dp
        )
        if fits:
            return fused(n_dp, n_own, *operands)
        return body(*operands)

    return jax.shard_map(step, mesh=mesh, in_specs=in_specs, out_specs=out_specs, check_vma=False)
```

```python
import functools

import jax
import jax.numpy as jnp
from jax import lax
from jax.experimental import pallas as pl
from jax.experimental.pallas import tpu as pltpu
from jax.sharding import PartitionSpec as P

decay_rate = 0.95
epsilon = 1e-06

MESH = pl.DeviceIdType.MESH
LANES = 128


def body(partial_grads, owner_list, left_stat, right_stat, left_root, right_root):
    owners = lax.axis_size("own")
    capacity = left_stat.shape[0]
    quarter = left_stat.shape[1]
    block_width = left_stat.shape[2]
    blocks = owner_list.shape[0]
    owner_hits = (owner_list[:, None] == jnp.arange(owners, dtype=jnp.int32)[None, :]).astype(
        jnp.int32
    )
    before = jnp.cumsum(owner_hits, axis=0) - owner_hits
    slot_index = jnp.sum(before * owner_hits, axis=1)
    slot_hits = (slot_index[:, None] == jnp.arange(capacity, dtype=jnp.int32)[None, :]).astype(
        jnp.int32
    )
    slot_match = slot_hits[:, :, None] * owner_hits[:, None, :]
    source_block = jnp.sum(slot_match * jnp.arange(blocks, dtype=jnp.int32)[:, None, None], axis=0)
    filled_flag = jnp.sum(slot_match, axis=0).astype(jnp.bfloat16)
    local_terms = partial_grads[0].astype(jnp.float32)
    shared = lax.psum(local_terms.astype(jnp.bfloat16), "dp")
    outgoing = jnp.take(shared, source_block, axis=0) * filled_flag[:, :, None, None]
    arrived = lax.all_to_all(outgoing, "own", split_axis=1, concat_axis=1, tiled=True)
    grad_part = arrived.reshape(capacity, block_width, arrived.shape[3])
    dp_lane = lax.axis_index("dp")
    own_index = lax.axis_index("own")
    owner_load = jnp.sum((owner_list == own_index).astype(jnp.int32))
    slot_used = (jnp.arange(capacity, dtype=jnp.int32) < owner_load)[:, None, None]
    row_start = dp_lane * quarter
    grad_rows = lax.dynamic_slice_in_dim(grad_part, row_start, quarter, 1)
    grad_colq = lax.dynamic_slice_in_dim(grad_part, row_start, quarter, 2)
    left_gram = jnp.einsum("cqk,cnk->cqn", grad_rows, grad_part, preferred_element_type=jnp.float32)
    right_gram = jnp.einsum(
        "ckq,ckn->cqn", grad_colq, grad_part, preferred_element_type=jnp.float32
    )
    new_left = jnp.where(slot_used, decay_rate * left_stat + left_gram / block_width, left_stat)
    new_right = jnp.where(slot_used, decay_rate * right_stat + right_gram / block_width, right_stat)
    half_done = jnp.einsum(
        "ckn,cqn->ckq", grad_part, right_root, preferred_element_type=jnp.float32
    ).astype(jnp.bfloat16)
    product = jnp.einsum(
        "cpn,cpq->cnq",
        lax.all_gather(left_root, "dp", axis=1, tiled=True),
        half_done,
        preferred_element_type=jnp.float32,
    )
    grad_sq = jnp.sum(jnp.square(grad_part.astype(jnp.float32)), axis=(1, 2))
    prod_sq = lax.psum(jnp.sum(product * product, axis=(1, 2)), "dp")
    cell_count = float(block_width * block_width)
    graft_ratio = jnp.sqrt(grad_sq / cell_count) / jnp.sqrt(prod_sq / cell_count + epsilon)
    scaled = (product * graft_ratio[:, None, None]).astype(jnp.bfloat16)
    returned = lax.all_to_all(
        scaled.reshape(capacity, owners, block_width // owners, quarter),
        "own",
        split_axis=1,
        concat_axis=1,
        tiled=True,
    )
    gathered_back = returned.reshape(capacity * owners, block_width // owners, quarter)
    update = jnp.take(gathered_back, slot_index * owners + owner_list, axis=0)
    return (new_left, new_right, update)


def kernel(
    n_dp,
    n_own,
    owner_ref,
    grads_ref,
    left_stat_ref,
    right_stat_ref,
    left_root_ref,
    right_root_ref,
    new_left_ref,
    new_right_ref,
    update_ref,
    parts,
    summed,
    routed,
    grad,
    left_full,
    right_quarter,
    left_old,
    right_old,
    sent_back,
    came_back,
    norm_sent,
    norm_came,
    ratio_all,
    local_sem,
    send_sem,
    recv_sem,
    spread_send,
    spread_recv,
):
    me = lax.axis_index("dp")
    own = lax.axis_index("own")
    blocks, _, rows, width = grads_ref.shape
    capacity, quarter, _ = left_stat_ref.shape
    per_quarter = n_own // n_dp
    dp_of = [me, me + 1 - 2 * (me % 2), me + 2 - 4 * (me // 2), 3 - me]
    near = n_own // 2
    base = (own // near) * near
    turn = own - base
    own_of = [base + lax.rem(turn + k, near) for k in range(near)]
    own_of += [near - base + lax.rem(turn + k, near) for k in range(near)]

    def send(src, dst, group, c, device):
        pltpu.make_async_remote_copy(
            src_ref=src,
            dst_ref=dst,
            send_sem=send_sem.at[group, c],
            recv_sem=recv_sem.at[group, c],
            device_id=device,
            device_id_type=MESH,
        ).start()

    def to_dp(k, src, dst, group, c):
        send(src, dst, group, c, (dp_of[k], own))

    def to_own(k, src, dst, group, c):
        send(src, dst, group, c, (me, own_of[k]))

    def wait_for(sem, like):
        pltpu.make_async_copy(like, like, sem).wait()

    sums, roots, routes_near, routes_far, norms, backs, ratios = range(7)
    sizes = {
        sums: parts.at[pl.ds(1, n_dp - 1)],
        roots: left_full.at[:, pl.ds(1, n_dp - 1), :, pl.ds(0, 2 * quarter)],
        routes_near: grad.at[0, pl.ds(1, near - 1), 0],
        routes_far: grad.at[0, pl.ds(0, near), 0],
        norms: norm_came.at[0, pl.ds(1, n_dp - 1)],
        backs: came_back.at[0, pl.ds(1, n_own - 1)],
        ratios: ratio_all.at[0, pl.ds(1, n_own - 1)],
    }

    def arrived(group, c=0):
        wait_for(recv_sem.at[group, c], sizes[group])

    local = [
        pltpu.make_async_copy(grads_ref.at[:, me], parts.at[0], local_sem.at[0]),
        pltpu.make_async_copy(right_root_ref, right_quarter, local_sem.at[1]),
        pltpu.make_async_copy(left_stat_ref, left_old, local_sem.at[2]),
        pltpu.make_async_copy(right_stat_ref, right_old, local_sem.at[3]),
    ]
    for k in range(n_dp):
        columns = pl.ds(pl.multiple_of(dp_of[k] * quarter, LANES), quarter)
        local.append(
            pltpu.make_async_copy(
                left_root_ref.at[:, :, columns],
                left_full.at[:, 0, :, pl.ds(k * quarter, quarter)],
                local_sem.at[4 + k],
            )
        )
    local[0].start()

    barrier = pltpu.get_barrier_semaphore()
    for k in range(1, n_dp):
        pl.semaphore_signal(barrier, inc=1, device_id=(dp_of[k], own), device_id_type=MESH)
    for k in range(1, n_own):
        pl.semaphore_signal(barrier, inc=1, device_id=(me, own_of[k]), device_id_type=MESH)
    pl.semaphore_wait(barrier, n_dp - 1 + n_own - 1)

    for k in reversed(range(1, n_dp)):
        to_dp(k, grads_ref.at[:, dp_of[k]], parts.at[k], sums, 0)

    def send_root(k, column, slots):
        columns = pl.ds(pl.multiple_of(dp_of[k ^ column] * quarter, LANES), quarter)
        to_dp(
            k,
            left_root_ref.at[slots, :, columns],
            left_full.at[slots, k, :, pl.ds(column * quarter, quarter)],
            roots,
            0,
        )

    every = pl.ds(0, capacity)
    root_pieces = [(1, 1, every), (2, 2, every), (3, 3, every), (1, 3, every), (2, 3, every)]
    root_pieces += [(1 + c % 2, 2 - c % 2, pl.ds(c, 1)) for c in range(capacity)]
    for copy in root_pieces[: n_dp - 1]:
        send_root(*copy)

    named = [owner_ref[b] for b in range(blocks)]
    slot_of = []
    for b in range(blocks):
        before = jnp.int32(0)
        for a in range(b):
            before += (named[a] == named[b]).astype(jnp.int32)
        slot_of.append(jnp.minimum(before, capacity - 1))
    source = {}
    filled = {}
    for k in range(n_own):
        for c in range(capacity):
            source[k, c] = jnp.int32(0)
            filled[k, c] = jnp.int32(0)
            for b in range(blocks):
                hit = jnp.logical_and(named[b] == own_of[k], slot_of[b] == c)
                source[k, c] = jnp.where(hit, jnp.int32(b), source[k, c])
                filled[k, c] = jnp.where(hit, jnp.int32(1), filled[k, c])

    local[0].wait()
    arrived(sums)
    total = parts[0].astype(jnp.float32)
    for k in range(1, n_dp):
        total += parts[k].astype(jnp.float32)
    summed[...] = total.astype(jnp.bfloat16)

    def pick(k, c):
        flag = filled[k, c].astype(jnp.float32)
        return (summed[source[k, c]].astype(jnp.float32) * flag).astype(jnp.bfloat16)

    for group, first, last in ((routes_near, 1, near), (routes_far, near, n_own)):
        for c in range(capacity):
            for k in range(first, last):
                routed[k, c] = pick(k, c)
                to_own(k, routed.at[k, c], grad.at[c, own, me], group, c)
    for c in range(capacity):
        grad[c, own, me] = pick(0, c)

    for copy in root_pieces[n_dp - 1 :]:
        send_root(*copy)
    for copy in local[1:]:
        copy.start()

    def half_of(c, far, at):
        start = near - base if far else base
        return grad.at[c, pl.ds(start, near), dp_of[at]]

    def spread(c, far, k, at):
        piece = half_of(c, far, at)
        across = k ^ at
        pltpu.make_async_remote_copy(
            src_ref=piece,
            dst_ref=piece,
            send_sem=spread_send.at[c, far, across],
            recv_sem=spread_recv.at[c, far, across],
            device_id=(dp_of[k], own),
            device_id_type=MESH,
        ).start()

    def first_to(c, far):
        return 1 + (c + far) % 2

    def spread_arrived(c, far, at):
        wait_for(spread_recv.at[c, far, at], half_of(c, far, at))

    def start_spread(c, far):
        arrived(routes_far if far else routes_near, c)
        first = first_to(c, far)
        spread(c, far, first, 0)
        spread(c, far, 3 - first, 0)

    def relay(c, far):
        came = first_to(c, far)
        spread_arrived(c, far, came)
        spread(c, far, 3 - came, came)

    halves = [(c, far) for far in range(2) for c in range(capacity)]
    lag = 2
    for at, half in enumerate(halves):
        start_spread(*half)
        if at >= lag:
            relay(*halves[at - lag])

    for copy in local[1:]:
        copy.wait()
    arrived(roots)
    for c in range(capacity):
        for i, j in ((0, 1), (0, 2), (0, 3), (1, 3), (2, 3), (1 + c % 2, 2 - c % 2)):
            left_full[c, j, :, pl.ds(i * quarter, quarter)] = left_full[
                c, i, :, pl.ds(j * quarter, quarter)
            ].T
    for half in halves[-lag:]:
        relay(*half)

    cells = float(width * width)
    nt = (((1,), (1,)), ((), ()))
    tn = (((0,), (0,)), ((), ()))

    def grad_rows(c, k):
        return grad[c, pl.ds(dp_of[k] * per_quarter, per_quarter)].reshape(quarter, width)

    def statistics(c):
        used = filled[0, c].astype(jnp.float32)
        decay = 1.0 - used * (1.0 - decay_rate)
        whole = grad[c].reshape(width, width)
        left_gram = lax.dot_general(
            grad_rows(c, 0), whole, nt, preferred_element_type=jnp.float32
        )
        new_left_ref[c] = decay * left_old[c] + left_gram * (1.0 / width)
        columns = pl.ds(pl.multiple_of(me * quarter, LANES), quarter)
        mine = grad[c, :, :, :, columns].reshape(width, quarter)
        right_gram = lax.dot_general(mine, whole, tn, preferred_element_type=jnp.float32)
        new_right_ref[c] = decay * right_old[c] + right_gram * (1.0 / width)

    for c in range(capacity):
        for far in range(2):
            spread_arrived(c, far, 3 - first_to(c, far))
            spread_arrived(c, far, 3)
        half = jnp.concatenate(
            [
                lax.dot_general(
                    grad_rows(c, k), right_quarter[c], nt, preferred_element_type=jnp.float32
                ).astype(jnp.bfloat16)
                for k in range(n_dp)
            ],
            axis=0,
        )
        product = jnp.dot(
            left_full[c].reshape(width, width), half, preferred_element_type=jnp.float32
        )
        for k in range(n_dp):
            piece = product[k * quarter : (k + 1) * quarter].astype(jnp.bfloat16)
            for j in range(per_quarter):
                step = quarter // per_quarter
                sent_back[c, dp_of[k] * per_quarter + j] = piece[j * step : (j + 1) * step]
        norm_sent[c] = jnp.sum(jnp.square(product).reshape(width // 8, 8, quarter), axis=0)
        for k in range(1, n_dp):
            to_dp(k, norm_sent.at[c], norm_came.at[c, k], norms, c)
        for k in reversed(range(1, n_own)):
            to_own(k, sent_back.at[c, own_of[k]], came_back.at[c, own], backs, c)
        came_back[c, own] = sent_back[c, own]
        squares = jnp.square(grad[c].reshape(width, width).astype(jnp.float32))
        grad_sq = jnp.sum(squares.reshape(width // 8, 8, width), axis=0)
        grad_all = jnp.sum(grad_sq, keepdims=True).reshape(1, 1)
        arrived(norms, c)
        prod_sq = norm_sent[c]
        for k in range(1, n_dp):
            prod_sq += norm_came[c, k]
        prod_all = jnp.sum(prod_sq, keepdims=True).reshape(1, 1)
        ratio = jnp.sqrt(grad_all / cells) / jnp.sqrt(prod_all / cells + epsilon)
        ratio_all[c, own] = jnp.broadcast_to(ratio, (8, LANES))
        for k in reversed(range(1, n_own)):
            to_own(k, ratio_all.at[c, own], ratio_all.at[c, own], ratios, c)
        statistics(c)


    for c in range(capacity):
        arrived(backs, c)
        arrived(ratios, c)
    for b in range(blocks):
        ratio = ratio_all[slot_of[b], named[b]][0:1, :]
        terms = came_back[slot_of[b], named[b]].astype(jnp.float32)
        update_ref[b] = (terms * ratio).astype(jnp.bfloat16)

    for group in sizes:
        for c in range(1 if group in (sums, roots) else capacity):
            wait_for(send_sem.at[group, c], sizes[group])
    for c, far in halves:
        for k in range(1, n_dp):
            wait_for(spread_send.at[c, far, k], half_of(c, far, 0))


def write_out(*refs):
    inputs, outputs, sems = refs[:3], refs[3:6], refs[6]
    copies = [
        pltpu.make_async_copy(inputs[i], outputs[i], sems.at[i]) for i in range(len(inputs))
    ]
    for copy in copies:
        copy.start()
    for copy in copies:
        copy.wait()


def fused(n_dp, n_own, partial_grads, owner_list, left_stat, right_stat, left_root, right_root):
    capacity, quarter, width = left_stat.shape
    blocks, strip = partial_grads.shape[1:3]
    rows = strip // n_dp
    bf16, f32 = jnp.bfloat16, jnp.float32
    dma = pltpu.SemaphoreType.DMA
    anywhere = pl.BlockSpec(memory_space=pl.ANY)
    hbm = functools.partial(pltpu.with_memory_space_constraint, memory_space=pltpu.HBM)
    shapes = (left_stat.shape, right_stat.shape, (blocks, strip, quarter))
    types = (f32, f32, bf16)
    results = pl.pallas_call(
        functools.partial(kernel, n_dp, n_own),
        out_shape=tuple(pltpu.VMEM(shape, kind) for shape, kind in zip(shapes, types)),
        in_specs=[pl.BlockSpec(memory_space=pltpu.SMEM)] + [anywhere] * 5,
        out_specs=tuple([pl.BlockSpec(memory_space=pltpu.VMEM)] * 3),
        scratch_shapes=[
            pltpu.VMEM((n_dp, blocks, rows, width), bf16),
            pltpu.VMEM((blocks, rows, width), bf16),
            pltpu.VMEM((n_own, capacity, rows, width), bf16),
            pltpu.VMEM((capacity, n_own, n_dp, rows, width), bf16),
            pltpu.VMEM((capacity, n_dp, quarter, width), bf16),
            pltpu.VMEM((capacity, quarter, width), bf16),
            pltpu.VMEM((capacity, quarter, width), f32),
            pltpu.VMEM((capacity, quarter, width), f32),
            pltpu.VMEM((capacity, n_own, strip, quarter), bf16),
            pltpu.VMEM((capacity, n_own, strip, quarter), bf16),
            pltpu.VMEM((capacity, 8, LANES), f32),
            pltpu.VMEM((capacity, n_dp, 8, LANES), f32),
            pltpu.VMEM((capacity, n_own, 8, LANES), f32),
            dma((4 + n_dp,)),
            dma((7, capacity)),
            dma((7, capacity)),
            dma((capacity, 2, n_dp)),
            dma((capacity, 2, n_dp)),
        ],
        compiler_params=pltpu.CompilerParams(
            collective_id=0, has_side_effects=True, vmem_limit_bytes=40 * 1024 * 1024
        ),
    )(
        hbm(owner_list),
        hbm(partial_grads[0].reshape(blocks, n_dp, rows, width)),
        hbm(left_stat),
        hbm(right_stat),
        hbm(left_root),
        hbm(right_root),
    )
    return pl.pallas_call(
        write_out,
        out_shape=tuple(jax.ShapeDtypeStruct(shape, kind) for shape, kind in zip(shapes, types)),
        in_specs=[anywhere] * 3,
        out_specs=tuple([pl.BlockSpec(memory_space=pltpu.HBM)] * 3),
        scratch_shapes=[dma((3,))],
        compiler_params=pltpu.CompilerParams(vmem_limit_bytes=4 * 1024 * 1024),
    )(*[pltpu.with_memory_space_constraint(x, pltpu.VMEM) for x in results])


def solution(mesh):
    n_dp, n_own = mesh.shape["dp"], mesh.shape["own"]
    in_specs = (
        P("dp", None, "own", None),
        P(),
        P("own", "dp", None),
        P("own", "dp", None),
        P("own", "dp", None),
        P("own", "dp", None),
    )
    out_specs = (P("own", "dp", None), P("own", "dp", None), P(None, "own", "dp"))

    def step(*operands):
        strip = operands[0].shape[2]
        quarter = operands[2].shape[1]
        fits = (
            n_dp == 4
            and n_own % n_dp == 0
            and n_own >= 2 * n_dp
            and strip % (16 * n_dp) == 0
            and quarter == LANES
            and strip * n_own == quarter * n_dp
        )
        if fits:
            return fused(n_dp, n_own, *operands)
        return body(*operands)

    return jax.shard_map(step, mesh=mesh, in_specs=in_specs, out_specs=out_specs, check_vma=False)
```

```python
import functools

import jax
import jax.numpy as jnp
from jax import lax
from jax.experimental import pallas as pl
from jax.experimental.pallas import tpu as pltpu
from jax.sharding import PartitionSpec as P

decay_rate = 0.95
epsilon = 1e-06

MESH = pl.DeviceIdType.MESH
LANES = 128


def body(partial_grads, owner_list, left_stat, right_stat, left_root, right_root):
    owners = lax.axis_size("own")
    capacity = left_stat.shape[0]
    quarter = left_stat.shape[1]
    block_width = left_stat.shape[2]
    blocks = owner_list.shape[0]
    owner_hits = (owner_list[:, None] == jnp.arange(owners, dtype=jnp.int32)[None, :]).astype(
        jnp.int32
    )
    before = jnp.cumsum(owner_hits, axis=0) - owner_hits
    slot_index = jnp.sum(before * owner_hits, axis=1)
    slot_hits = (slot_index[:, None] == jnp.arange(capacity, dtype=jnp.int32)[None, :]).astype(
        jnp.int32
    )
    slot_match = slot_hits[:, :, None] * owner_hits[:, None, :]
    source_block = jnp.sum(slot_match * jnp.arange(blocks, dtype=jnp.int32)[:, None, None], axis=0)
    filled_flag = jnp.sum(slot_match, axis=0).astype(jnp.bfloat16)
    local_terms = partial_grads[0].astype(jnp.float32)
    shared = lax.psum(local_terms.astype(jnp.bfloat16), "dp")
    outgoing = jnp.take(shared, source_block, axis=0) * filled_flag[:, :, None, None]
    arrived = lax.all_to_all(outgoing, "own", split_axis=1, concat_axis=1, tiled=True)
    grad_part = arrived.reshape(capacity, block_width, arrived.shape[3])
    dp_lane = lax.axis_index("dp")
    own_index = lax.axis_index("own")
    owner_load = jnp.sum((owner_list == own_index).astype(jnp.int32))
    slot_used = (jnp.arange(capacity, dtype=jnp.int32) < owner_load)[:, None, None]
    row_start = dp_lane * quarter
    grad_rows = lax.dynamic_slice_in_dim(grad_part, row_start, quarter, 1)
    grad_colq = lax.dynamic_slice_in_dim(grad_part, row_start, quarter, 2)
    left_gram = jnp.einsum("cqk,cnk->cqn", grad_rows, grad_part, preferred_element_type=jnp.float32)
    right_gram = jnp.einsum(
        "ckq,ckn->cqn", grad_colq, grad_part, preferred_element_type=jnp.float32
    )
    new_left = jnp.where(slot_used, decay_rate * left_stat + left_gram / block_width, left_stat)
    new_right = jnp.where(slot_used, decay_rate * right_stat + right_gram / block_width, right_stat)
    half_done = jnp.einsum(
        "ckn,cqn->ckq", grad_part, right_root, preferred_element_type=jnp.float32
    ).astype(jnp.bfloat16)
    product = jnp.einsum(
        "cpn,cpq->cnq",
        lax.all_gather(left_root, "dp", axis=1, tiled=True),
        half_done,
        preferred_element_type=jnp.float32,
    )
    grad_sq = jnp.sum(jnp.square(grad_part.astype(jnp.float32)), axis=(1, 2))
    prod_sq = lax.psum(jnp.sum(product * product, axis=(1, 2)), "dp")
    cell_count = float(block_width * block_width)
    graft_ratio = jnp.sqrt(grad_sq / cell_count) / jnp.sqrt(prod_sq / cell_count + epsilon)
    scaled = (product * graft_ratio[:, None, None]).astype(jnp.bfloat16)
    returned = lax.all_to_all(
        scaled.reshape(capacity, owners, block_width // owners, quarter),
        "own",
        split_axis=1,
        concat_axis=1,
        tiled=True,
    )
    gathered_back = returned.reshape(capacity * owners, block_width // owners, quarter)
    update = jnp.take(gathered_back, slot_index * owners + owner_list, axis=0)
    return (new_left, new_right, update)


def kernel(
    n_dp,
    n_own,
    owner_ref,
    grads_ref,
    left_stat_ref,
    right_stat_ref,
    left_root_ref,
    right_root_ref,
    new_left_ref,
    new_right_ref,
    update_ref,
    parts,
    summed,
    routed,
    grad,
    left_full,
    right_quarter,
    left_old,
    right_old,
    sent_back,
    came_back,
    norm_sent,
    norm_came,
    ratio_all,
    local_sem,
    send_sem,
    recv_sem,
    spread_send,
    spread_recv,
):
    me = lax.axis_index("dp")
    own = lax.axis_index("own")
    blocks, _, rows, width = grads_ref.shape
    capacity, quarter, _ = left_stat_ref.shape
    per_quarter = n_own // n_dp
    dp_of = [me, me + 1 - 2 * (me % 2), me + 2 - 4 * (me // 2), 3 - me]
    near = n_own // 2
    base = (own // near) * near
    turn = own - base
    own_of = [base + lax.rem(turn + k, near) for k in range(near)]
    own_of += [near - base + lax.rem(turn + k, near) for k in range(near)]

    def send(src, dst, group, c, device):
        pltpu.make_async_remote_copy(
            src_ref=src,
            dst_ref=dst,
            send_sem=send_sem.at[group, c],
            recv_sem=recv_sem.at[group, c],
            device_id=device,
            device_id_type=MESH,
        ).start()

    def to_dp(k, src, dst, group, c):
        send(src, dst, group, c, (dp_of[k], own))

    def to_own(k, src, dst, group, c):
        send(src, dst, group, c, (me, own_of[k]))

    def wait_for(sem, like):
        pltpu.make_async_copy(like, like, sem).wait()

    sums, roots, routes_near, routes_far, norms, backs, ratios = range(7)
    sizes = {
        sums: parts.at[pl.ds(1, n_dp - 1)],
        roots: left_full.at[:, pl.ds(1, n_dp - 1), :, pl.ds(0, 2 * quarter)],
        routes_near: grad.at[0, pl.ds(1, near - 1), 0],
        routes_far: grad.at[0, pl.ds(0, near), 0],
        norms: norm_came.at[0, pl.ds(1, n_dp - 1)],
        backs: came_back.at[0, pl.ds(1, n_own - 1)],
        ratios: ratio_all.at[0, pl.ds(1, n_own - 1)],
    }

    def arrived(group, c=0):
        wait_for(recv_sem.at[group, c], sizes[group])

    local = [
        pltpu.make_async_copy(grads_ref.at[:, me], parts.at[0], local_sem.at[0]),
        pltpu.make_async_copy(right_root_ref, right_quarter, local_sem.at[1]),
        pltpu.make_async_copy(left_stat_ref, left_old, local_sem.at[2]),
        pltpu.make_async_copy(right_stat_ref, right_old, local_sem.at[3]),
    ]
    for k in range(n_dp):
        columns = pl.ds(pl.multiple_of(dp_of[k] * quarter, LANES), quarter)
        local.append(
            pltpu.make_async_copy(
                left_root_ref.at[:, :, columns],
                left_full.at[:, 0, :, pl.ds(k * quarter, quarter)],
                local_sem.at[4 + k],
            )
        )
    local[0].start()

    barrier = pltpu.get_barrier_semaphore()
    for k in range(1, n_dp):
        pl.semaphore_signal(barrier, inc=1, device_id=(dp_of[k], own), device_id_type=MESH)
    for k in range(1, n_own):
        pl.semaphore_signal(barrier, inc=1, device_id=(me, own_of[k]), device_id_type=MESH)
    pl.semaphore_wait(barrier, n_dp - 1 + n_own - 1)

    for k in reversed(range(1, n_dp)):
        to_dp(k, grads_ref.at[:, dp_of[k]], parts.at[k], sums, 0)

    def send_root(k, column, slots):
        columns = pl.ds(pl.multiple_of(dp_of[k ^ column] * quarter, LANES), quarter)
        to_dp(
            k,
            left_root_ref.at[slots, :, columns],
            left_full.at[slots, k, :, pl.ds(column * quarter, quarter)],
            roots,
            0,
        )

    every = pl.ds(0, capacity)
    root_pieces = [(1, 1, every), (2, 2, every), (3, 3, every), (1, 3, every), (2, 3, every)]
    root_pieces += [(1 + c % 2, 2 - c % 2, pl.ds(c, 1)) for c in range(capacity)]
    for copy in root_pieces[: n_dp - 1]:
        send_root(*copy)

    named = [owner_ref[b] for b in range(blocks)]
    slot_of = []
    for b in range(blocks):
        before = jnp.int32(0)
        for a in range(b):
            before += (named[a] == named[b]).astype(jnp.int32)
        slot_of.append(jnp.minimum(before, capacity - 1))
    source = {}
    filled = {}
    for k in range(n_own):
        for c in range(capacity):
            source[k, c] = jnp.int32(0)
            filled[k, c] = jnp.int32(0)
            for b in range(blocks):
                hit = jnp.logical_and(named[b] == own_of[k], slot_of[b] == c)
                source[k, c] = jnp.where(hit, jnp.int32(b), source[k, c])
                filled[k, c] = jnp.where(hit, jnp.int32(1), filled[k, c])

    local[0].wait()
    arrived(sums)
    total = parts[0].astype(jnp.float32)
    for k in range(1, n_dp):
        total += parts[k].astype(jnp.float32)
    summed[...] = total.astype(jnp.bfloat16)

    def pick(k, c):
        flag = filled[k, c].astype(jnp.float32)
        return (summed[source[k, c]].astype(jnp.float32) * flag).astype(jnp.bfloat16)

    for group, first, last in ((routes_near, 1, near), (routes_far, near, n_own)):
        for c in range(capacity):
            for k in range(first, last):
                routed[k, c] = pick(k, c)
                to_own(k, routed.at[k, c], grad.at[c, own, me], group, c)
    for c in range(capacity):
        grad[c, own, me] = pick(0, c)

    for copy in root_pieces[n_dp - 1 :]:
        send_root(*copy)
    for copy in local[4:] + local[1:4]:
        copy.start()

    def half_of(c, far, at):
        start = near - base if far else base
        return grad.at[c, pl.ds(start, near), dp_of[at]]

    def spread(c, far, k, at):
        piece = half_of(c, far, at)
        across = k ^ at
        pltpu.make_async_remote_copy(
            src_ref=piece,
            dst_ref=piece,
            send_sem=spread_send.at[c, far, across],
            recv_sem=spread_recv.at[c, far, across],
            device_id=(dp_of[k], own),
            device_id_type=MESH,
        ).start()

    def first_to(c, far):
        return 1 + (c + far) % 2

    def spread_arrived(c, far, at):
        wait_for(spread_recv.at[c, far, at], half_of(c, far, at))

    def start_spread(c, far):
        arrived(routes_far if far else routes_near, c)
        first = first_to(c, far)
        spread(c, far, first, 0)
        spread(c, far, 3 - first, 0)

    def relay(c, far):
        came = first_to(c, far)
        spread_arrived(c, far, came)
        spread(c, far, 3 - came, came)

    for c in range(capacity):
        start_spread(c, 0)

    for copy in local[4:] + local[1:2]:
        copy.wait()
    arrived(roots)
    for c in range(capacity):
        for i, j in ((0, 1), (0, 2), (0, 3), (1, 3), (2, 3), (1 + c % 2, 2 - c % 2)):
            left_full[c, j, :, pl.ds(i * quarter, quarter)] = left_full[
                c, i, :, pl.ds(j * quarter, quarter)
            ].T

    for c in range(capacity):
        start_spread(c, 1)
        relay(c, 0)
    for c in range(capacity):
        relay(c, 1)

    cells = float(width * width)
    nt = (((1,), (1,)), ((), ()))
    tn = (((0,), (0,)), ((), ()))

    def grad_rows(c, k):
        return grad[c, pl.ds(dp_of[k] * per_quarter, per_quarter)].reshape(quarter, width)

    def statistics(c):
        used = filled[0, c].astype(jnp.float32)
        decay = 1.0 - used * (1.0 - decay_rate)
        whole = grad[c].reshape(width, width)
        left_gram = lax.dot_general(
            grad_rows(c, 0), whole, nt, preferred_element_type=jnp.float32
        )
        new_left_ref[c] = decay * left_old[c] + left_gram * (1.0 / width)
        columns = pl.ds(pl.multiple_of(me * quarter, LANES), quarter)
        mine = grad[c, :, :, :, columns].reshape(width, quarter)
        right_gram = lax.dot_general(mine, whole, tn, preferred_element_type=jnp.float32)
        new_right_ref[c] = decay * right_old[c] + right_gram * (1.0 / width)

    for c in range(capacity):
        for far in range(2):
            spread_arrived(c, far, 3 - first_to(c, far))
            spread_arrived(c, far, 3)
        half = jnp.concatenate(
            [
                lax.dot_general(
                    grad_rows(c, k), right_quarter[c], nt, preferred_element_type=jnp.float32
                ).astype(jnp.bfloat16)
                for k in range(n_dp)
            ],
            axis=0,
        )
        product = jnp.dot(
            left_full[c].reshape(width, width), half, preferred_element_type=jnp.float32
        )
        for k in range(n_dp):
            piece = product[k * quarter : (k + 1) * quarter].astype(jnp.bfloat16)
            for j in range(per_quarter):
                step = quarter // per_quarter
                sent_back[c, dp_of[k] * per_quarter + j] = piece[j * step : (j + 1) * step]
        norm_sent[c] = jnp.sum(jnp.square(product).reshape(width // 8, 8, quarter), axis=0)
        for k in range(1, n_dp):
            to_dp(k, norm_sent.at[c], norm_came.at[c, k], norms, c)
        for k in reversed(range(1, n_own)):
            to_own(k, sent_back.at[c, own_of[k]], came_back.at[c, own], backs, c)
        came_back[c, own] = sent_back[c, own]

    for c in range(capacity):
        squares = jnp.square(grad[c].reshape(width, width).astype(jnp.float32))
        grad_sq = jnp.sum(squares.reshape(width // 8, 8, width), axis=0)
        grad_all = jnp.sum(grad_sq, keepdims=True).reshape(1, 1)
        arrived(norms, c)
        prod_sq = norm_sent[c]
        for k in range(1, n_dp):
            prod_sq += norm_came[c, k]
        prod_all = jnp.sum(prod_sq, keepdims=True).reshape(1, 1)
        ratio = jnp.sqrt(grad_all / cells) / jnp.sqrt(prod_all / cells + epsilon)
        ratio_all[c, own] = jnp.broadcast_to(ratio, (8, LANES))
        for k in reversed(range(1, n_own)):
            to_own(k, ratio_all.at[c, own], ratio_all.at[c, own], ratios, c)
    local[2].wait()
    local[3].wait()
    for c in range(capacity):
        statistics(c)

    for c in range(capacity):
        arrived(backs, c)
        arrived(ratios, c)
    for b in range(blocks):
        ratio = ratio_all[slot_of[b], named[b]][0:1, :]
        terms = came_back[slot_of[b], named[b]].astype(jnp.float32)
        update_ref[b] = (terms * ratio).astype(jnp.bfloat16)

    for group in sizes:
        for c in range(1 if group in (sums, roots) else capacity):
            wait_for(send_sem.at[group, c], sizes[group])
    for c in range(capacity):
        for far in range(2):
            for k in range(1, n_dp):
                wait_for(spread_send.at[c, far, k], half_of(c, far, 0))


def write_out(*refs):
    inputs, outputs, sems = refs[:3], refs[3:6], refs[6]
    copies = [
        pltpu.make_async_copy(inputs[i], outputs[i], sems.at[i]) for i in range(len(inputs))
    ]
    for copy in copies:
        copy.start()
    for copy in copies:
        copy.wait()


def fused(n_dp, n_own, partial_grads, owner_list, left_stat, right_stat, left_root, right_root):
    capacity, quarter, width = left_stat.shape
    blocks, strip = partial_grads.shape[1:3]
    rows = strip // n_dp
    bf16, f32 = jnp.bfloat16, jnp.float32
    dma = pltpu.SemaphoreType.DMA
    anywhere = pl.BlockSpec(memory_space=pl.ANY)
    hbm = functools.partial(pltpu.with_memory_space_constraint, memory_space=pltpu.HBM)
    shapes = (left_stat.shape, right_stat.shape, (blocks, strip, quarter))
    types = (f32, f32, bf16)
    results = pl.pallas_call(
        functools.partial(kernel, n_dp, n_own),
        out_shape=tuple(pltpu.VMEM(shape, kind) for shape, kind in zip(shapes, types)),
        in_specs=[pl.BlockSpec(memory_space=pltpu.SMEM)] + [anywhere] * 5,
        out_specs=tuple([pl.BlockSpec(memory_space=pltpu.VMEM)] * 3),
        scratch_shapes=[
            pltpu.VMEM((n_dp, blocks, rows, width), bf16),
            pltpu.VMEM((blocks, rows, width), bf16),
            pltpu.VMEM((n_own, capacity, rows, width), bf16),
            pltpu.VMEM((capacity, n_own, n_dp, rows, width), bf16),
            pltpu.VMEM((capacity, n_dp, quarter, width), bf16),
            pltpu.VMEM((capacity, quarter, width), bf16),
            pltpu.VMEM((capacity, quarter, width), f32),
            pltpu.VMEM((capacity, quarter, width), f32),
            pltpu.VMEM((capacity, n_own, strip, quarter), bf16),
            pltpu.VMEM((capacity, n_own, strip, quarter), bf16),
            pltpu.VMEM((capacity, 8, LANES), f32),
            pltpu.VMEM((capacity, n_dp, 8, LANES), f32),
            pltpu.VMEM((capacity, n_own, 8, LANES), f32),
            dma((4 + n_dp,)),
            dma((7, capacity)),
            dma((7, capacity)),
            dma((capacity, 2, n_dp)),
            dma((capacity, 2, n_dp)),
        ],
        compiler_params=pltpu.CompilerParams(
            collective_id=0, has_side_effects=True, vmem_limit_bytes=40 * 1024 * 1024
        ),
    )(
        hbm(owner_list),
        hbm(partial_grads[0].reshape(blocks, n_dp, rows, width)),
        hbm(left_stat),
        hbm(right_stat),
        hbm(left_root),
        hbm(right_root),
    )
    return pl.pallas_call(
        write_out,
        out_shape=tuple(jax.ShapeDtypeStruct(shape, kind) for shape, kind in zip(shapes, types)),
        in_specs=[anywhere] * 3,
        out_specs=tuple([pl.BlockSpec(memory_space=pltpu.HBM)] * 3),
        scratch_shapes=[dma((3,))],
        compiler_params=pltpu.CompilerParams(vmem_limit_bytes=4 * 1024 * 1024),
    )(*[pltpu.with_memory_space_constraint(x, pltpu.VMEM) for x in results])


def solution(mesh):
    n_dp, n_own = mesh.shape["dp"], mesh.shape["own"]
    in_specs = (
        P("dp", None, "own", None),
        P(),
        P("own", "dp", None),
        P("own", "dp", None),
        P("own", "dp", None),
        P("own", "dp", None),
    )
    out_specs = (P("own", "dp", None), P("own", "dp", None), P(None, "own", "dp"))

    def step(*operands):
        strip = operands[0].shape[2]
        quarter = operands[2].shape[1]
        fits = (
            n_dp == 4
            and n_own % n_dp == 0
            and n_own >= 2 * n_dp
            and strip % (16 * n_dp) == 0
            and quarter == LANES
            and strip * n_own == quarter * n_dp
        )
        if fits:
            return fused(n_dp, n_own, *operands)
        return body(*operands)

    return jax.shard_map(step, mesh=mesh, in_specs=in_specs, out_specs=out_specs, check_vma=False)
```

```python
import functools

import jax
import jax.numpy as jnp
from jax import lax
from jax.experimental import pallas as pl
from jax.experimental.pallas import tpu as pltpu
from jax.sharding import PartitionSpec as P

decay_rate = 0.95
epsilon = 1e-06

MESH = pl.DeviceIdType.MESH
LANES = 128


def body(partial_grads, owner_list, left_stat, right_stat, left_root, right_root):
    owners = lax.axis_size("own")
    capacity = left_stat.shape[0]
    quarter = left_stat.shape[1]
    block_width = left_stat.shape[2]
    blocks = owner_list.shape[0]
    owner_hits = (owner_list[:, None] == jnp.arange(owners, dtype=jnp.int32)[None, :]).astype(
        jnp.int32
    )
    before = jnp.cumsum(owner_hits, axis=0) - owner_hits
    slot_index = jnp.sum(before * owner_hits, axis=1)
    slot_hits = (slot_index[:, None] == jnp.arange(capacity, dtype=jnp.int32)[None, :]).astype(
        jnp.int32
    )
    slot_match = slot_hits[:, :, None] * owner_hits[:, None, :]
    source_block = jnp.sum(slot_match * jnp.arange(blocks, dtype=jnp.int32)[:, None, None], axis=0)
    filled_flag = jnp.sum(slot_match, axis=0).astype(jnp.bfloat16)
    local_terms = partial_grads[0].astype(jnp.float32)
    shared = lax.psum(local_terms.astype(jnp.bfloat16), "dp")
    outgoing = jnp.take(shared, source_block, axis=0) * filled_flag[:, :, None, None]
    arrived = lax.all_to_all(outgoing, "own", split_axis=1, concat_axis=1, tiled=True)
    grad_part = arrived.reshape(capacity, block_width, arrived.shape[3])
    dp_lane = lax.axis_index("dp")
    own_index = lax.axis_index("own")
    owner_load = jnp.sum((owner_list == own_index).astype(jnp.int32))
    slot_used = (jnp.arange(capacity, dtype=jnp.int32) < owner_load)[:, None, None]
    row_start = dp_lane * quarter
    grad_rows = lax.dynamic_slice_in_dim(grad_part, row_start, quarter, 1)
    grad_colq = lax.dynamic_slice_in_dim(grad_part, row_start, quarter, 2)
    left_gram = jnp.einsum("cqk,cnk->cqn", grad_rows, grad_part, preferred_element_type=jnp.float32)
    right_gram = jnp.einsum(
        "ckq,ckn->cqn", grad_colq, grad_part, preferred_element_type=jnp.float32
    )
    new_left = jnp.where(slot_used, decay_rate * left_stat + left_gram / block_width, left_stat)
    new_right = jnp.where(slot_used, decay_rate * right_stat + right_gram / block_width, right_stat)
    half_done = jnp.einsum(
        "ckn,cqn->ckq", grad_part, right_root, preferred_element_type=jnp.float32
    ).astype(jnp.bfloat16)
    product = jnp.einsum(
        "cpn,cpq->cnq",
        lax.all_gather(left_root, "dp", axis=1, tiled=True),
        half_done,
        preferred_element_type=jnp.float32,
    )
    grad_sq = jnp.sum(jnp.square(grad_part.astype(jnp.float32)), axis=(1, 2))
    prod_sq = lax.psum(jnp.sum(product * product, axis=(1, 2)), "dp")
    cell_count = float(block_width * block_width)
    graft_ratio = jnp.sqrt(grad_sq / cell_count) / jnp.sqrt(prod_sq / cell_count + epsilon)
    scaled = (product * graft_ratio[:, None, None]).astype(jnp.bfloat16)
    returned = lax.all_to_all(
        scaled.reshape(capacity, owners, block_width // owners, quarter),
        "own",
        split_axis=1,
        concat_axis=1,
        tiled=True,
    )
    gathered_back = returned.reshape(capacity * owners, block_width // owners, quarter)
    update = jnp.take(gathered_back, slot_index * owners + owner_list, axis=0)
    return (new_left, new_right, update)


def kernel(
    n_dp,
    n_own,
    owner_ref,
    grads_ref,
    left_stat_ref,
    right_stat_ref,
    left_root_ref,
    right_root_ref,
    new_left_ref,
    new_right_ref,
    update_ref,
    parts,
    summed,
    routed,
    grad,
    left_full,
    right_quarter,
    left_old,
    right_old,
    sent_back,
    came_back,
    norm_sent,
    norm_came,
    ratio_all,
    local_sem,
    send_sem,
    recv_sem,
    spread_send,
    spread_recv,
):
    me = lax.axis_index("dp")
    own = lax.axis_index("own")
    blocks, _, rows, width = grads_ref.shape
    capacity, quarter, _ = left_stat_ref.shape
    per_quarter = n_own // n_dp
    dp_of = [me, me + 1 - 2 * (me % 2), me + 2 - 4 * (me // 2), 3 - me]
    near = n_own // 2
    base = (own // near) * near
    turn = own - base
    own_of = [base + lax.rem(turn + k, near) for k in range(near)]
    own_of += [near - base + lax.rem(turn + k, near) for k in range(near)]

    def send(src, dst, group, c, device):
        pltpu.make_async_remote_copy(
            src_ref=src,
            dst_ref=dst,
            send_sem=send_sem.at[group, c],
            recv_sem=recv_sem.at[group, c],
            device_id=device,
            device_id_type=MESH,
        ).start()

    def to_dp(k, src, dst, group, c):
        send(src, dst, group, c, (dp_of[k], own))

    def to_own(k, src, dst, group, c):
        send(src, dst, group, c, (me, own_of[k]))

    def wait_for(sem, like):
        pltpu.make_async_copy(like, like, sem).wait()

    sums, roots, routes_near, routes_far, norms, backs, ratios = range(7)
    roots_x, roots_y, roots_across = range(7, 10)
    sizes = {
        sums: parts.at[pl.ds(1, n_dp - 1)],
        roots: left_full.at[:, pl.ds(1, n_dp - 1), :, pl.ds(0, quarter)],
        roots_x: left_full.at[:, 1, :, pl.ds(0, quarter)],
        roots_y: left_full.at[:, 2, :, pl.ds(0, quarter)],
        roots_across: left_full.at[:, 3, :, pl.ds(0, quarter)],
        routes_near: grad.at[0, pl.ds(1, near - 1), 0],
        routes_far: grad.at[0, pl.ds(0, near), 0],
        norms: norm_came.at[0, pl.ds(1, n_dp - 1)],
        backs: came_back.at[0, pl.ds(1, n_own - 1)],
        ratios: ratio_all.at[0, pl.ds(1, n_own - 1)],
    }

    def arrived(group, c=0):
        wait_for(recv_sem.at[group, c], sizes[group])

    local = [
        pltpu.make_async_copy(grads_ref.at[:, me], parts.at[0], local_sem.at[0]),
        pltpu.make_async_copy(right_root_ref, right_quarter, local_sem.at[1]),
        pltpu.make_async_copy(left_stat_ref, left_old, local_sem.at[2]),
        pltpu.make_async_copy(right_stat_ref, right_old, local_sem.at[3]),
    ]
    for k in range(n_dp):
        columns = pl.ds(pl.multiple_of(dp_of[k] * quarter, LANES), quarter)
        local.append(
            pltpu.make_async_copy(
                left_root_ref.at[:, :, columns],
                left_full.at[:, 0, :, pl.ds(k * quarter, quarter)],
                local_sem.at[4 + k],
            )
        )
    local[0].start()

    barrier = pltpu.get_barrier_semaphore()
    for k in range(1, n_dp):
        pl.semaphore_signal(barrier, inc=1, device_id=(dp_of[k], own), device_id_type=MESH)
    for k in range(1, n_own):
        pl.semaphore_signal(barrier, inc=1, device_id=(me, own_of[k]), device_id_type=MESH)
    pl.semaphore_wait(barrier, n_dp - 1 + n_own - 1)

    for k in reversed(range(1, n_dp)):
        to_dp(k, grads_ref.at[:, dp_of[k]], parts.at[k], sums, 0)

    def send_root(k, column, slots, group):
        columns = pl.ds(pl.multiple_of(dp_of[k ^ column] * quarter, LANES), quarter)
        to_dp(
            k,
            left_root_ref.at[slots, :, columns],
            left_full.at[slots, k, :, pl.ds(column * quarter, quarter)],
            group,
            0,
        )

    every = pl.ds(0, capacity)
    root_pieces = [(1, 1, every, roots_x), (2, 2, every, roots_y)]
    root_pieces += [(1, 3, every, roots), (2, 3, every, roots)]
    root_pieces += [(1 + c % 2, 2 - c % 2, pl.ds(c, 1), roots) for c in range(capacity)]
    for copy in root_pieces[:3]:
        send_root(*copy)

    named = [owner_ref[b] for b in range(blocks)]
    slot_of = []
    for b in range(blocks):
        before = jnp.int32(0)
        for a in range(b):
            before += (named[a] == named[b]).astype(jnp.int32)
        slot_of.append(jnp.minimum(before, capacity - 1))
    source = {}
    filled = {}
    for k in range(n_own):
        for c in range(capacity):
            source[k, c] = jnp.int32(0)
            filled[k, c] = jnp.int32(0)
            for b in range(blocks):
                hit = jnp.logical_and(named[b] == own_of[k], slot_of[b] == c)
                source[k, c] = jnp.where(hit, jnp.int32(b), source[k, c])
                filled[k, c] = jnp.where(hit, jnp.int32(1), filled[k, c])

    local[0].wait()
    arrived(sums)
    total = parts[0].astype(jnp.float32)
    for k in range(1, n_dp):
        total += parts[k].astype(jnp.float32)
    summed[...] = total.astype(jnp.bfloat16)

    def pick(k, c):
        flag = filled[k, c].astype(jnp.float32)
        return (summed[source[k, c]].astype(jnp.float32) * flag).astype(jnp.bfloat16)

    for group, first, last in ((routes_near, 1, near), (routes_far, near, n_own)):
        for c in range(capacity):
            for k in range(first, last):
                routed[k, c] = pick(k, c)
                to_own(k, routed.at[k, c], grad.at[c, own, me], group, c)
    for c in range(capacity):
        grad[c, own, me] = pick(0, c)

    for copy in root_pieces[3:]:
        send_root(*copy)
    for copy in local[4:] + local[1:4]:
        copy.start()

    def half_of(c, far, at):
        start = near - base if far else base
        return grad.at[c, pl.ds(start, near), dp_of[at]]

    def spread(c, far, k, at):
        piece = half_of(c, far, at)
        across = k ^ at
        pltpu.make_async_remote_copy(
            src_ref=piece,
            dst_ref=piece,
            send_sem=spread_send.at[c, far, across],
            recv_sem=spread_recv.at[c, far, across],
            device_id=(dp_of[k], own),
            device_id_type=MESH,
        ).start()

    def first_to(c, far):
        return 1 + (c + far) % 2

    def spread_arrived(c, far, at):
        wait_for(spread_recv.at[c, far, at], half_of(c, far, at))

    def start_spread(c, far):
        arrived(routes_far if far else routes_near, c)
        first = first_to(c, far)
        spread(c, far, first, 0)
        spread(c, far, 3 - first, 0)

    def relay(c, far):
        came = first_to(c, far)
        spread_arrived(c, far, came)
        spread(c, far, 3 - came, came)

    start_spread(0, 0)
    arrived(roots_x)
    arrived(roots_y)
    for c in range(capacity):
        came = 1 + c % 2
        to_dp(
            3 - came,
            left_full.at[c, came, :, pl.ds(came * quarter, quarter)],
            left_full.at[c, 3, :, pl.ds(3 * quarter, quarter)],
            roots_across,
            0,
        )
    for c in range(1, capacity):
        start_spread(c, 0)

    for copy in local[4:] + local[1:2]:
        copy.wait()
    arrived(roots)
    for c in range(capacity):
        for i, j in ((0, 1), (0, 2), (0, 3), (1, 3), (2, 3), (1 + c % 2, 2 - c % 2)):
            left_full[c, j, :, pl.ds(i * quarter, quarter)] = left_full[
                c, i, :, pl.ds(j * quarter, quarter)
            ].T

    for c in range(capacity):
        start_spread(c, 1)
        relay(c, 0)
    for c in range(capacity):
        relay(c, 1)

    cells = float(width * width)
    nt = (((1,), (1,)), ((), ()))
    tn = (((0,), (0,)), ((), ()))

    def grad_rows(c, k):
        return grad[c, pl.ds(dp_of[k] * per_quarter, per_quarter)].reshape(quarter, width)

    def statistics(c):
        used = filled[0, c].astype(jnp.float32)
        decay = 1.0 - used * (1.0 - decay_rate)
        whole = grad[c].reshape(width, width)
        left_gram = lax.dot_general(
            grad_rows(c, 0), whole, nt, preferred_element_type=jnp.float32
        )
        new_left_ref[c] = decay * left_old[c] + left_gram * (1.0 / width)
        columns = pl.ds(pl.multiple_of(me * quarter, LANES), quarter)
        mine = grad[c, :, :, :, columns].reshape(width, quarter)
        right_gram = lax.dot_general(mine, whole, tn, preferred_element_type=jnp.float32)
        new_right_ref[c] = decay * right_old[c] + right_gram * (1.0 / width)

    arrived(roots_across)
    for c in range(capacity):
        for far in range(2):
            spread_arrived(c, far, 3 - first_to(c, far))
            spread_arrived(c, far, 3)
        half = jnp.concatenate(
            [
                lax.dot_general(
                    grad_rows(c, k), right_quarter[c], nt, preferred_element_type=jnp.float32
                ).astype(jnp.bfloat16)
                for k in range(n_dp)
            ],
            axis=0,
        )
        product = jnp.dot(
            left_full[c].reshape(width, width), half, preferred_element_type=jnp.float32
        )
        for k in range(n_dp):
            piece = product[k * quarter : (k + 1) * quarter].astype(jnp.bfloat16)
            for j in range(per_quarter):
                step = quarter // per_quarter
                sent_back[c, dp_of[k] * per_quarter + j] = piece[j * step : (j + 1) * step]
        norm_sent[c] = jnp.sum(jnp.square(product).reshape(width // 8, 8, quarter), axis=0)
        for k in range(1, n_dp):
            to_dp(k, norm_sent.at[c], norm_came.at[c, k], norms, c)
        for k in reversed(range(1, n_own)):
            to_own(k, sent_back.at[c, own_of[k]], came_back.at[c, own], backs, c)
        came_back[c, own] = sent_back[c, own]

    for c in range(capacity):
        squares = jnp.square(grad[c].reshape(width, width).astype(jnp.float32))
        grad_sq = jnp.sum(squares.reshape(width // 8, 8, width), axis=0)
        grad_all = jnp.sum(grad_sq, keepdims=True).reshape(1, 1)
        arrived(norms, c)
        prod_sq = norm_sent[c]
        for k in range(1, n_dp):
            prod_sq += norm_came[c, k]
        prod_all = jnp.sum(prod_sq, keepdims=True).reshape(1, 1)
        ratio = jnp.sqrt(grad_all / cells) / jnp.sqrt(prod_all / cells + epsilon)
        ratio_all[c, own] = jnp.broadcast_to(ratio, (8, LANES))
        for k in reversed(range(1, n_own)):
            to_own(k, ratio_all.at[c, own], ratio_all.at[c, own], ratios, c)
    local[2].wait()
    local[3].wait()
    for c in range(capacity):
        statistics(c)

    for c in range(capacity):
        arrived(backs, c)
        arrived(ratios, c)
    for b in range(blocks):
        ratio = ratio_all[slot_of[b], named[b]][0:1, :]
        terms = came_back[slot_of[b], named[b]].astype(jnp.float32)
        update_ref[b] = (terms * ratio).astype(jnp.bfloat16)

    for group in sizes:
        for c in range(capacity if group in (routes_near, routes_far, norms, backs, ratios) else 1):
            wait_for(send_sem.at[group, c], sizes[group])
    for c in range(capacity):
        for far in range(2):
            for k in range(1, n_dp):
                wait_for(spread_send.at[c, far, k], half_of(c, far, 0))


def write_out(*refs):
    inputs, outputs, sems = refs[:3], refs[3:6], refs[6]
    copies = []
    for i, parts in enumerate((4, 4, 2)):
        size = inputs[i].shape[0] * inputs[i].shape[1] // parts
        step = min(size, inputs[i].shape[1])
        deep = size // step
        for part in range(parts):
            first, row = divmod(part * size, inputs[i].shape[1])
            piece = (pl.ds(first, deep), pl.ds(row, step))
            copies.append(
                pltpu.make_async_copy(
                    inputs[i].at[piece], outputs[i].at[piece], sems.at[len(copies)]
                )
            )
    for copy in copies:
        copy.start()
    for copy in copies:
        copy.wait()


def fused(n_dp, n_own, partial_grads, owner_list, left_stat, right_stat, left_root, right_root):
    capacity, quarter, width = left_stat.shape
    blocks, strip = partial_grads.shape[1:3]
    rows = strip // n_dp
    bf16, f32 = jnp.bfloat16, jnp.float32
    dma = pltpu.SemaphoreType.DMA
    anywhere = pl.BlockSpec(memory_space=pl.ANY)
    hbm = functools.partial(pltpu.with_memory_space_constraint, memory_space=pltpu.HBM)
    shapes = (left_stat.shape, right_stat.shape, (blocks, strip, quarter))
    types = (f32, f32, bf16)
    results = pl.pallas_call(
        functools.partial(kernel, n_dp, n_own),
        out_shape=tuple(pltpu.VMEM(shape, kind) for shape, kind in zip(shapes, types)),
        in_specs=[pl.BlockSpec(memory_space=pltpu.SMEM)] + [anywhere] * 5,
        out_specs=tuple([pl.BlockSpec(memory_space=pltpu.VMEM)] * 3),
        scratch_shapes=[
            pltpu.VMEM((n_dp, blocks, rows, width), bf16),
            pltpu.VMEM((blocks, rows, width), bf16),
            pltpu.VMEM((n_own, capacity, rows, width), bf16),
            pltpu.VMEM((capacity, n_own, n_dp, rows, width), bf16),
            pltpu.VMEM((capacity, n_dp, quarter, width), bf16),
            pltpu.VMEM((capacity, quarter, width), bf16),
            pltpu.VMEM((capacity, quarter, width), f32),
            pltpu.VMEM((capacity, quarter, width), f32),
            pltpu.VMEM((capacity, n_own, strip, quarter), bf16),
            pltpu.VMEM((capacity, n_own, strip, quarter), bf16),
            pltpu.VMEM((capacity, 8, LANES), f32),
            pltpu.VMEM((capacity, n_dp, 8, LANES), f32),
            pltpu.VMEM((capacity, n_own, 8, LANES), f32),
            dma((4 + n_dp,)),
            dma((10, capacity)),
            dma((10, capacity)),
            dma((capacity, 2, n_dp)),
            dma((capacity, 2, n_dp)),
        ],
        compiler_params=pltpu.CompilerParams(
            collective_id=0, has_side_effects=True, vmem_limit_bytes=40 * 1024 * 1024
        ),
    )(
        hbm(owner_list),
        hbm(partial_grads[0].reshape(blocks, n_dp, rows, width)),
        hbm(left_stat),
        hbm(right_stat),
        hbm(left_root),
        hbm(right_root),
    )
    return pl.pallas_call(
        write_out,
        out_shape=tuple(jax.ShapeDtypeStruct(shape, kind) for shape, kind in zip(shapes, types)),
        in_specs=[anywhere] * 3,
        out_specs=tuple([pl.BlockSpec(memory_space=pltpu.HBM)] * 3),
        scratch_shapes=[dma((10,))],
        compiler_params=pltpu.CompilerParams(vmem_limit_bytes=4 * 1024 * 1024),
    )(*[pltpu.with_memory_space_constraint(x, pltpu.VMEM) for x in results])


def solution(mesh):
    n_dp, n_own = mesh.shape["dp"], mesh.shape["own"]
    in_specs = (
        P("dp", None, "own", None),
        P(),
        P("own", "dp", None),
        P("own", "dp", None),
        P("own", "dp", None),
        P("own", "dp", None),
    )
    out_specs = (P("own", "dp", None), P("own", "dp", None), P(None, "own", "dp"))

    def step(*operands):
        strip = operands[0].shape[2]
        quarter = operands[2].shape[1]
        fits = (
            n_dp == 4
            and n_own % n_dp == 0
            and n_own >= 2 * n_dp
            and strip % (16 * n_dp) == 0
            and quarter == LANES
            and strip * n_own == quarter * n_dp
        )
        if fits:
            return fused(n_dp, n_own, *operands)
        return body(*operands)

    return jax.shard_map(step, mesh=mesh, in_specs=in_specs, out_specs=out_specs, check_vma=False)
```

```python
import functools

import jax
import jax.numpy as jnp
from jax import lax
from jax.experimental import pallas as pl
from jax.experimental.pallas import tpu as pltpu
from jax.sharding import PartitionSpec as P

decay_rate = 0.95
epsilon = 1e-06

MESH = pl.DeviceIdType.MESH
LANES = 128


def body(partial_grads, owner_list, left_stat, right_stat, left_root, right_root):
    owners = lax.axis_size("own")
    capacity = left_stat.shape[0]
    quarter = left_stat.shape[1]
    block_width = left_stat.shape[2]
    blocks = owner_list.shape[0]
    owner_hits = (owner_list[:, None] == jnp.arange(owners, dtype=jnp.int32)[None, :]).astype(
        jnp.int32
    )
    before = jnp.cumsum(owner_hits, axis=0) - owner_hits
    slot_index = jnp.sum(before * owner_hits, axis=1)
    slot_hits = (slot_index[:, None] == jnp.arange(capacity, dtype=jnp.int32)[None, :]).astype(
        jnp.int32
    )
    slot_match = slot_hits[:, :, None] * owner_hits[:, None, :]
    source_block = jnp.sum(slot_match * jnp.arange(blocks, dtype=jnp.int32)[:, None, None], axis=0)
    filled_flag = jnp.sum(slot_match, axis=0).astype(jnp.bfloat16)
    local_terms = partial_grads[0].astype(jnp.float32)
    shared = lax.psum(local_terms.astype(jnp.bfloat16), "dp")
    outgoing = jnp.take(shared, source_block, axis=0) * filled_flag[:, :, None, None]
    arrived = lax.all_to_all(outgoing, "own", split_axis=1, concat_axis=1, tiled=True)
    grad_part = arrived.reshape(capacity, block_width, arrived.shape[3])
    dp_lane = lax.axis_index("dp")
    own_index = lax.axis_index("own")
    owner_load = jnp.sum((owner_list == own_index).astype(jnp.int32))
    slot_used = (jnp.arange(capacity, dtype=jnp.int32) < owner_load)[:, None, None]
    row_start = dp_lane * quarter
    grad_rows = lax.dynamic_slice_in_dim(grad_part, row_start, quarter, 1)
    grad_colq = lax.dynamic_slice_in_dim(grad_part, row_start, quarter, 2)
    left_gram = jnp.einsum("cqk,cnk->cqn", grad_rows, grad_part, preferred_element_type=jnp.float32)
    right_gram = jnp.einsum(
        "ckq,ckn->cqn", grad_colq, grad_part, preferred_element_type=jnp.float32
    )
    new_left = jnp.where(slot_used, decay_rate * left_stat + left_gram / block_width, left_stat)
    new_right = jnp.where(slot_used, decay_rate * right_stat + right_gram / block_width, right_stat)
    half_done = jnp.einsum(
        "ckn,cqn->ckq", grad_part, right_root, preferred_element_type=jnp.float32
    ).astype(jnp.bfloat16)
    product = jnp.einsum(
        "cpn,cpq->cnq",
        lax.all_gather(left_root, "dp", axis=1, tiled=True),
        half_done,
        preferred_element_type=jnp.float32,
    )
    grad_sq = jnp.sum(jnp.square(grad_part.astype(jnp.float32)), axis=(1, 2))
    prod_sq = lax.psum(jnp.sum(product * product, axis=(1, 2)), "dp")
    cell_count = float(block_width * block_width)
    graft_ratio = jnp.sqrt(grad_sq / cell_count) / jnp.sqrt(prod_sq / cell_count + epsilon)
    scaled = (product * graft_ratio[:, None, None]).astype(jnp.bfloat16)
    returned = lax.all_to_all(
        scaled.reshape(capacity, owners, block_width // owners, quarter),
        "own",
        split_axis=1,
        concat_axis=1,
        tiled=True,
    )
    gathered_back = returned.reshape(capacity * owners, block_width // owners, quarter)
    update = jnp.take(gathered_back, slot_index * owners + owner_list, axis=0)
    return (new_left, new_right, update)


def kernel(
    n_dp,
    n_own,
    owner_ref,
    grads_ref,
    left_stat_ref,
    right_stat_ref,
    left_root_ref,
    right_root_ref,
    new_left_ref,
    new_right_ref,
    update_ref,
    parts,
    summed,
    routed,
    grad,
    left_full,
    right_quarter,
    left_old,
    right_old,
    sent_back,
    came_back,
    norm_sent,
    norm_came,
    ratio_all,
    half_rows,
    local_sem,
    send_sem,
    recv_sem,
    spread_send,
    spread_recv,
):
    me = lax.axis_index("dp")
    own = lax.axis_index("own")
    blocks, _, rows, width = grads_ref.shape
    capacity, quarter, _ = left_stat_ref.shape
    per_quarter = n_own // n_dp
    dp_of = [me, me + 1 - 2 * (me % 2), me + 2 - 4 * (me // 2), 3 - me]
    near = n_own // 2
    base = (own // near) * near
    turn = own - base
    own_of = [base + lax.rem(turn + k, near) for k in range(near)]
    own_of += [near - base + lax.rem(turn + k, near) for k in range(near)]

    def send(src, dst, group, c, device):
        pltpu.make_async_remote_copy(
            src_ref=src,
            dst_ref=dst,
            send_sem=send_sem.at[group, c],
            recv_sem=recv_sem.at[group, c],
            device_id=device,
            device_id_type=MESH,
        ).start()

    def to_dp(k, src, dst, group, c):
        send(src, dst, group, c, (dp_of[k], own))

    def to_own(k, src, dst, group, c):
        send(src, dst, group, c, (me, own_of[k]))

    def wait_for(sem, like):
        pltpu.make_async_copy(like, like, sem).wait()

    sums, roots, routes_near, routes_far, norms, backs, ratios = range(7)
    sizes = {
        sums: parts.at[pl.ds(1, n_dp - 1)],
        roots: left_full.at[:, pl.ds(1, n_dp - 1), :, pl.ds(0, 2 * quarter)],
        routes_near: grad.at[0, pl.ds(1, near - 1), 0],
        routes_far: grad.at[0, pl.ds(0, near), 0],
        norms: norm_came.at[0, pl.ds(1, n_dp - 1)],
        backs: came_back.at[0, pl.ds(1, n_own - 1)],
        ratios: ratio_all.at[0, pl.ds(1, n_own - 1)],
    }

    def arrived(group, c=0):
        wait_for(recv_sem.at[group, c], sizes[group])

    local = [
        pltpu.make_async_copy(grads_ref.at[:, me], parts.at[0], local_sem.at[0]),
        pltpu.make_async_copy(right_root_ref, right_quarter, local_sem.at[1]),
        pltpu.make_async_copy(left_stat_ref, left_old, local_sem.at[2]),
        pltpu.make_async_copy(right_stat_ref, right_old, local_sem.at[3]),
    ]
    for k in range(n_dp):
        columns = pl.ds(pl.multiple_of(dp_of[k] * quarter, LANES), quarter)
        local.append(
            pltpu.make_async_copy(
                left_root_ref.at[:, :, columns],
                left_full.at[:, 0, :, pl.ds(k * quarter, quarter)],
                local_sem.at[4 + k],
            )
        )
    local[0].start()

    barrier = pltpu.get_barrier_semaphore()
    for k in reversed(range(1, n_own)):
        pl.semaphore_signal(barrier, inc=1, device_id=(me, own_of[k]), device_id_type=MESH)
    for k in reversed(range(1, n_dp)):
        pl.semaphore_signal(barrier, inc=1, device_id=(dp_of[k], own), device_id_type=MESH)
    pl.semaphore_wait(barrier, n_dp - 1 + n_own - 1)

    for k in reversed(range(1, n_dp)):
        to_dp(k, grads_ref.at[:, dp_of[k]], parts.at[k], sums, 0)

    def send_root(k, column, slots):
        columns = pl.ds(pl.multiple_of(dp_of[k ^ column] * quarter, LANES), quarter)
        to_dp(
            k,
            left_root_ref.at[slots, :, columns],
            left_full.at[slots, k, :, pl.ds(column * quarter, quarter)],
            roots,
            0,
        )

    every = pl.ds(0, capacity)
    root_pieces = [(1, 1, every), (2, 2, every), (3, 3, every), (1, 3, every), (2, 3, every)]
    root_pieces += [(1 + c % 2, 2 - c % 2, pl.ds(c, 1)) for c in range(capacity)]
    for copy in root_pieces[: n_dp - 1]:
        send_root(*copy)

    named = [owner_ref[b] for b in range(blocks)]
    slot_of = []
    for b in range(blocks):
        before = jnp.int32(0)
        for a in range(b):
            before += (named[a] == named[b]).astype(jnp.int32)
        slot_of.append(jnp.minimum(before, capacity - 1))
    source = {}
    filled = {}
    for k in range(n_own):
        for c in range(capacity):
            source[k, c] = jnp.int32(0)
            filled[k, c] = jnp.int32(0)
            for b in range(blocks):
                hit = jnp.logical_and(named[b] == own_of[k], slot_of[b] == c)
                source[k, c] = jnp.where(hit, jnp.int32(b), source[k, c])
                filled[k, c] = jnp.where(hit, jnp.int32(1), filled[k, c])

    local[0].wait()
    arrived(sums)
    total = parts[0].astype(jnp.float32)
    for k in range(1, n_dp):
        total += parts[k].astype(jnp.float32)
    summed[...] = total.astype(jnp.bfloat16)

    def pick(k, c):
        flag = filled[k, c].astype(jnp.float32)
        return (summed[source[k, c]].astype(jnp.float32) * flag).astype(jnp.bfloat16)

    for group, first, last in ((routes_near, 1, near), (routes_far, near, n_own)):
        for c in range(capacity):
            for k in range(first, last):
                routed[k, c] = pick(k, c)
                to_own(k, routed.at[k, c], grad.at[c, own, me], group, c)
    for c in range(capacity):
        grad[c, own, me] = pick(0, c)

    for copy in root_pieces[n_dp - 1 :]:
        send_root(*copy)
    for copy in local[4:] + local[1:4]:
        copy.start()

    def half_of(c, far, at):
        start = near - base if far else base
        return grad.at[c, pl.ds(start, near), dp_of[at]]

    def spread(c, far, k, at):
        piece = half_of(c, far, at)
        across = k ^ at
        pltpu.make_async_remote_copy(
            src_ref=piece,
            dst_ref=piece,
            send_sem=spread_send.at[c, far, across],
            recv_sem=spread_recv.at[c, far, across],
            device_id=(dp_of[k], own),
            device_id_type=MESH,
        ).start()

    def first_to(c, far):
        return 1 + (c + far) % 2

    def spread_arrived(c, far, at):
        wait_for(spread_recv.at[c, far, at], half_of(c, far, at))

    def start_spread(c, far):
        arrived(routes_far if far else routes_near, c)
        first = first_to(c, far)
        spread(c, far, first, 0)
        spread(c, far, 3 - first, 0)

    def relay(c, far):
        came = first_to(c, far)
        spread_arrived(c, far, came)
        spread(c, far, 3 - came, came)

    for c in range(capacity):
        start_spread(c, 0)

    for copy in local[4:] + local[1:2]:
        copy.wait()
    arrived(roots)
    for c in range(capacity):
        for i, j in ((0, 1), (0, 2), (0, 3), (1, 3), (2, 3), (1 + c % 2, 2 - c % 2)):
            left_full[c, j, :, pl.ds(i * quarter, quarter)] = left_full[
                c, i, :, pl.ds(j * quarter, quarter)
            ].T

    for c in range(capacity):
        start_spread(c, 1)
        relay(c, 0)
    for c in range(capacity):
        relay(c, 1)

    cells = float(width * width)
    nt = (((1,), (1,)), ((), ()))
    tn = (((0,), (0,)), ((), ()))

    def grad_rows(c, k):
        return grad[c, pl.ds(dp_of[k] * per_quarter, per_quarter)].reshape(quarter, width)

    def statistics(c):
        used = filled[0, c].astype(jnp.float32)
        decay = 1.0 - used * (1.0 - decay_rate)
        whole = grad[c].reshape(width, width)
        left_gram = lax.dot_general(
            grad_rows(c, 0), whole, nt, preferred_element_type=jnp.float32
        )
        new_left_ref[c] = decay * left_old[c] + left_gram * (1.0 / width)
        columns = pl.ds(pl.multiple_of(me * quarter, LANES), quarter)
        mine = grad[c, :, :, :, columns].reshape(width, quarter)
        right_gram = lax.dot_general(mine, whole, tn, preferred_element_type=jnp.float32)
        new_right_ref[c] = decay * right_old[c] + right_gram * (1.0 / width)

    for c in range(capacity):
        for far in range(2):
            spread_arrived(c, far, 3 - first_to(c, far))
            spread_arrived(c, far, 3)
            first = (near - base if far else base) // per_quarter
            for i in range(near // per_quarter):
                piece = grad[c, pl.ds((first + i) * per_quarter, per_quarter)]
                half_rows[c, first + i] = lax.dot_general(
                    piece.reshape(quarter, width),
                    right_quarter[c],
                    nt,
                    preferred_element_type=jnp.float32,
                ).astype(jnp.bfloat16)
        half = jnp.concatenate([half_rows[c, dp_of[k]] for k in range(n_dp)], axis=0)
        product = jnp.dot(
            left_full[c].reshape(width, width), half, preferred_element_type=jnp.float32
        )
        for k in range(n_dp):
            piece = product[k * quarter : (k + 1) * quarter].astype(jnp.bfloat16)
            for j in range(per_quarter):
                step = quarter // per_quarter
                sent_back[c, dp_of[k] * per_quarter + j] = piece[j * step : (j + 1) * step]
        norm_sent[c] = jnp.sum(jnp.square(product).reshape(width // 8, 8, quarter), axis=0)
        for k in range(1, n_dp):
            to_dp(k, norm_sent.at[c], norm_came.at[c, k], norms, c)
        for k in reversed(range(1, n_own)):
            to_own(k, sent_back.at[c, own_of[k]], came_back.at[c, own], backs, c)
        came_back[c, own] = sent_back[c, own]

    for c in range(capacity):
        squares = jnp.square(grad[c].reshape(width, width).astype(jnp.float32))
        grad_sq = jnp.sum(squares.reshape(width // 8, 8, width), axis=0)
        grad_all = jnp.sum(grad_sq, keepdims=True).reshape(1, 1)
        arrived(norms, c)
        prod_sq = norm_sent[c]
        for k in range(1, n_dp):
            prod_sq += norm_came[c, k]
        prod_all = jnp.sum(prod_sq, keepdims=True).reshape(1, 1)
        ratio = jnp.sqrt(grad_all / cells) / jnp.sqrt(prod_all / cells + epsilon)
        ratio_all[c, own] = jnp.broadcast_to(ratio, (8, LANES))
        for k in reversed(range(1, n_own)):
            to_own(k, ratio_all.at[c, own], ratio_all.at[c, own], ratios, c)
    local[2].wait()
    local[3].wait()
    for c in range(capacity):
        statistics(c)

    for c in range(capacity):
        arrived(backs, c)
        arrived(ratios, c)
    for b in range(blocks):
        ratio = ratio_all[slot_of[b], named[b]][0:1, :]
        terms = came_back[slot_of[b], named[b]].astype(jnp.float32)
        update_ref[b] = (terms * ratio).astype(jnp.bfloat16)

    for group in sizes:
        for c in range(1 if group in (sums, roots) else capacity):
            wait_for(send_sem.at[group, c], sizes[group])
    for c in range(capacity):
        for far in range(2):
            for k in range(1, n_dp):
                wait_for(spread_send.at[c, far, k], half_of(c, far, 0))


def write_out(*refs):
    inputs, outputs, sems = refs[:3], refs[3:6], refs[6]
    copies = [
        pltpu.make_async_copy(inputs[i], outputs[i], sems.at[i]) for i in range(len(inputs))
    ]
    for copy in copies:
        copy.start()
    for copy in copies:
        copy.wait()


def fused(n_dp, n_own, partial_grads, owner_list, left_stat, right_stat, left_root, right_root):
    capacity, quarter, width = left_stat.shape
    blocks, strip = partial_grads.shape[1:3]
    rows = strip // n_dp
    bf16, f32 = jnp.bfloat16, jnp.float32
    dma = pltpu.SemaphoreType.DMA
    anywhere = pl.BlockSpec(memory_space=pl.ANY)
    hbm = functools.partial(pltpu.with_memory_space_constraint, memory_space=pltpu.HBM)
    shapes = (left_stat.shape, right_stat.shape, (blocks, strip, quarter))
    types = (f32, f32, bf16)
    results = pl.pallas_call(
        functools.partial(kernel, n_dp, n_own),
        out_shape=tuple(pltpu.VMEM(shape, kind) for shape, kind in zip(shapes, types)),
        in_specs=[pl.BlockSpec(memory_space=pltpu.SMEM)] + [anywhere] * 5,
        out_specs=tuple([pl.BlockSpec(memory_space=pltpu.VMEM)] * 3),
        scratch_shapes=[
            pltpu.VMEM((n_dp, blocks, rows, width), bf16),
            pltpu.VMEM((blocks, rows, width), bf16),
            pltpu.VMEM((n_own, capacity, rows, width), bf16),
            pltpu.VMEM((capacity, n_own, n_dp, rows, width), bf16),
            pltpu.VMEM((capacity, n_dp, quarter, width), bf16),
            pltpu.VMEM((capacity, quarter, width), bf16),
            pltpu.VMEM((capacity, quarter, width), f32),
            pltpu.VMEM((capacity, quarter, width), f32),
            pltpu.VMEM((capacity, n_own, strip, quarter), bf16),
            pltpu.VMEM((capacity, n_own, strip, quarter), bf16),
            pltpu.VMEM((capacity, 8, LANES), f32),
            pltpu.VMEM((capacity, n_dp, 8, LANES), f32),
            pltpu.VMEM((capacity, n_own, 8, LANES), f32),
            pltpu.VMEM((capacity, n_dp, quarter, quarter), bf16),
            dma((4 + n_dp,)),
            dma((7, capacity)),
            dma((7, capacity)),
            dma((capacity, 2, n_dp)),
            dma((capacity, 2, n_dp)),
        ],
        compiler_params=pltpu.CompilerParams(
            collective_id=0, has_side_effects=True, vmem_limit_bytes=40 * 1024 * 1024
        ),
    )(
        hbm(owner_list),
        hbm(partial_grads[0].reshape(blocks, n_dp, rows, width)),
        hbm(left_stat),
        hbm(right_stat),
        hbm(left_root),
        hbm(right_root),
    )
    return pl.pallas_call(
        write_out,
        out_shape=tuple(jax.ShapeDtypeStruct(shape, kind) for shape, kind in zip(shapes, types)),
        in_specs=[anywhere] * 3,
        out_specs=tuple([pl.BlockSpec(memory_space=pltpu.HBM)] * 3),
        scratch_shapes=[dma((3,))],
        compiler_params=pltpu.CompilerParams(vmem_limit_bytes=4 * 1024 * 1024),
    )(*[pltpu.with_memory_space_constraint(x, pltpu.VMEM) for x in results])


def solution(mesh):
    n_dp, n_own = mesh.shape["dp"], mesh.shape["own"]
    in_specs = (
        P("dp", None, "own", None),
        P(),
        P("own", "dp", None),
        P("own", "dp", None),
        P("own", "dp", None),
        P("own", "dp", None),
    )
    out_specs = (P("own", "dp", None), P("own", "dp", None), P(None, "own", "dp"))

    def step(*operands):
        strip = operands[0].shape[2]
        quarter = operands[2].shape[1]
        fits = (
            n_dp == 4
            and n_own % n_dp == 0
            and n_own >= 2 * n_dp
            and strip % (16 * n_dp) == 0
            and quarter == LANES
            and strip * n_own == quarter * n_dp
        )
        if fits:
            return fused(n_dp, n_own, *operands)
        return body(*operands)

    return jax.shard_map(step, mesh=mesh, in_specs=in_specs, out_specs=out_specs, check_vma=False)
```
